128 devices in a mesh: dp: 2 (over core), expert: 64 (over z, x, y).
Axes of the slice: x: 4, y: 4, z: 4, core: 2. Of those that a mesh axis runs over, the one named last changes fastest.
Arguments:
- tokens: bfloat16 [16384, 2048], P(('dp', 'expert')), may hold values from -6 to 6
- cotangent: bfloat16 [16384, 2048], P(('dp', 'expert')), may hold values from -6 to 6
- routes: int32 [16384, 8], P(('dp', 'expert')), may hold values from 0 to 63, all different within a row
- route_weight: int32 [16384, 8], P(('dp', 'expert')), may hold values from 1 to 4096
- replica_pick: int32 [16384, 8], P(('dp', 'expert')), may hold values 0 or 1
- hot_experts: int32 [8], replicated, may hold values from 0 to 63, as said below
- hot_holders: int32 [8], replicated, may hold values from 1 to 62, as said below
- capacity: int32 [64], replicated, may hold values from 6 to 8
- gate_weight: bfloat16 [64, 2048, 768], P('expert'), may hold values from -0.125 to 0.125
- up_weight: bfloat16 [64, 2048, 768], P('expert'), may hold values from -0.125 to 0.125
- down_weight: bfloat16 [64, 2048, 768], P('expert'), may hold values from -0.21875 to 0.21875
Outputs:
- mixed: bfloat16 [16384, 2048], P(('dp', 'expert'))
- grad_tokens: bfloat16 [16384, 2048], P(('dp', 'expert'))
- grad_gate: bfloat16 [64, 2048, 768], P('expert', 'dp')
- grad_up: bfloat16 [64, 2048, 768], P('expert', 'dp')
- grad_down: bfloat16 [64, 2048, 768], P('expert', 'dp')
The draws below stay inside these ranges and needn't reach their ends.
Inputs may be any that keep to these rules, and one draw needn't show every extreme that they name: `hot_experts`: 8 distinct experts. 8 distinct indices along expert, none of them equal to an entry of hot_experts; the device at hot_holders[j] holds the replica of hot_experts[j].
All inputs are finite; a program needn't handle non-finite values. No bound on the sum of `replica_pick` on one device may be relied on, other than what follows from the above.
Results may differ from the reference program's by a relative error of at most 0.0095.
Values may be sent and summed in bfloat16 or wider, within the bound.
No kernel may reach another device: no remote copies, remote signals or barrier semaphores. Data moves between devices by JAX's collectives and lax.ppermute only.
A program may use at most 192 MiB of HBM per device.

```python
import jax
import jax.numpy as jnp
from jax import lax

D = 2048
FF = 768
TOPK = 8
HOT = 8
CAP = 8
RCAP = 3
TOK_DEV = 128
EXPERTS = 64
TOKENS = 16384
N_DP = 2
N_EXPERT = 64


def hot_order(key):
    middle = (jax.random.permutation(key, EXPERTS - 4) + 2).astype(jnp.int32)
    first_ends = jnp.array([0, EXPERTS - 1], jnp.int32)
    second_ends = jnp.array([1, EXPERTS - 2], jnp.int32)
    return jnp.concatenate([first_ends, middle[:HOT - 2], second_ends, middle[HOT - 2:]])


def draw_hot_experts(key, part):
    ordered = hot_order(key)
    key = jax.random.fold_in(key, 1)
    return jax.random.permutation(key, ordered[:HOT]).astype(jnp.int32)


def draw_hot_holders(key, part):
    ordered = hot_order(key)
    key = jax.random.fold_in(key, 2)
    return jax.random.permutation(key, ordered[HOT:2 * HOT]).astype(jnp.int32)


def draw_capacity(key, part):
    ordered = hot_order(key)
    key = jax.random.fold_in(key, 3)
    values = jax.random.randint(key, (EXPERTS,), CAP - 2, CAP + 1)
    values = values.at[ordered[0]].set(CAP)
    values = values.at[ordered[HOT]].set(CAP - 2)
    return values.astype(jnp.int32)


def plant(values, rng, smallest, top_value):
    spot = [jax.random.randint(jax.random.fold_in(rng, axis), (), 0, length) for axis, length in enumerate(values.shape)]
    widest = values.shape.index(max(values.shape))
    neighbour = spot[:widest] + [(spot[widest] + 1) % values.shape[widest]] + spot[widest + 1:]
    return values.at[tuple(spot)].set(smallest).at[tuple(neighbour)].set(top_value)


def levels(rng, extent, pieces, low, largest):
    loudness = 1.0
    for dim, parts in pieces:
        heights = jax.random.uniform(jax.random.fold_in(jax.random.fold_in(rng, 6), dim), (parts,), jnp.float32, low / len(pieces), largest / len(pieces))
        loudness = loudness * jnp.repeat(jnp.exp(heights), extent[dim] // parts).reshape((-1,) + (1,) * (len(extent) - 1 - dim))
    return loudness


def choose_distinct(rng, rows, amount, top, lift):
    sequence = jax.random.permutation(jax.random.fold_in(rng, 1), amount)
    favour = sequence
    for power in range(3):
        favour = favour * favour // amount
    favour = favour * lift // amount
    tickets = jax.random.randint(jax.random.fold_in(rng, 2), (rows, amount), 0, 4096) + favour
    fixed_rows = jax.random.permutation(jax.random.fold_in(rng, 3), rows)[jnp.arange(amount) % rows]
    tickets = jnp.where(jnp.arange(rows)[:, None] == fixed_rows[None, :], 1 << 14, tickets)
    score = tickets * amount + jnp.arange(amount)
    return lax.top_k(score.astype(jnp.int32), top)[1].astype(jnp.int32)


def centred(key, dims, scale, limit, shards=(), held_as=jnp.bfloat16):
    values = jax.random.normal(key, dims, jnp.float32) * scale
    if len(shards) > 0:
        values = levels(key, dims, shards, -0.22, 0.18) * values
    return jnp.clip(values, min=-limit, max=limit).astype(held_as)


def setup_inputs(seed: int = 0) -> dict:
    streams_of = jax.random.split(jax.random.key(seed), 12)
    return {
        "tokens": centred(streams_of[0], (TOKENS, D), 1.0, 6.0, ((0, 128),)),
        "cotangent": centred(streams_of[1], (TOKENS, D), 1.0, 6.0, ((0, 128),)),
        "routes": choose_distinct(streams_of[2], TOKENS, EXPERTS, TOPK, 2048),
        "route_weight": plant(jax.random.randint(streams_of[3], (TOKENS, TOPK), 1, 4097), jax.random.fold_in(streams_of[3], 1), 1, 4096).astype(jnp.int32),
        "replica_pick": plant((jax.random.randint(streams_of[4], (TOKENS, TOPK), 0, 2) < 1).astype(jnp.int32), jax.random.fold_in(streams_of[4], 1), 0, 1),
        "hot_experts": draw_hot_experts(jax.random.fold_in(streams_of[11], 71), 0),
        "hot_holders": draw_hot_holders(jax.random.fold_in(streams_of[11], 71), 0),
        "capacity": draw_capacity(jax.random.fold_in(streams_of[11], 71), 0),
        "gate_weight": centred(streams_of[8], (EXPERTS, D, FF), D ** -0.5, 0.125, ((0, 64),)),
        "up_weight": centred(streams_of[9], (EXPERTS, D, FF), D ** -0.5, 0.125, ((0, 64),)),
        "down_weight": centred(streams_of[10], (EXPERTS, D, FF), FF ** -0.5, 0.21875, ((0, 64),)),
    }


def plan_routes(flat_experts, flat_pick, hot_experts, hot_holders, capacity):
    experts = capacity.shape[0]
    matches = flat_experts[:, None] == hot_experts[None, :]
    replica = jnp.logical_and(jnp.any(matches, axis=1), flat_pick == 1)
    holder = jnp.sum(jnp.where(matches, hot_holders[None, :], 0), axis=1).astype(jnp.int32)
    labels = flat_experts + experts * replica.astype(jnp.int32)
    classes = jnp.arange(2 * experts, dtype=jnp.int32)
    onehot = (labels[:, None] == classes[None, :]).astype(jnp.int32)
    ranking = jnp.sum((jnp.cumsum(onehot, axis=0) - onehot) * onehot, axis=1).astype(jnp.int32)
    expert_ids = jnp.arange(experts, dtype=jnp.int32)
    cap_home = jnp.sum(jnp.where(flat_experts[:, None] == expert_ids[None, :], capacity[None, :], 0), axis=1).astype(jnp.int32)
    cap_holder = jnp.sum(jnp.where(holder[:, None] == expert_ids[None, :], capacity[None, :], 0), axis=1).astype(jnp.int32)
    limits = jnp.where(replica, jnp.minimum(cap_holder, RCAP), cap_home)
    kept_mask = ranking < limits
    slot_index = (ranking + CAP * replica.astype(jnp.int32)).astype(jnp.int32)
    return replica, holder, kept_mask, slot_index


def expert_rows(row_data, grads_in, gate_w, up_w, down_w):
    pre_gate = jnp.dot(row_data, gate_w, preferred_element_type=jnp.float32)
    pre_up = jnp.dot(row_data, up_w, preferred_element_type=jnp.float32)
    sigma = jax.nn.sigmoid(pre_gate)
    active = pre_gate * sigma
    hidden = (active * pre_up).astype(jnp.bfloat16)
    output = jnp.dot(hidden, down_w.T, preferred_element_type=jnp.float32).astype(jnp.bfloat16)
    back_hidden = jnp.dot(grads_in, down_w, preferred_element_type=jnp.float32)
    back_gate = (back_hidden * pre_up * sigma * (1.0 + pre_gate * (1.0 - sigma))).astype(jnp.bfloat16)
    back_up = (back_hidden * active).astype(jnp.bfloat16)
    back_rows = (jnp.dot(back_gate, gate_w.T, preferred_element_type=jnp.float32)
                 + jnp.dot(back_up, up_w.T, preferred_element_type=jnp.float32)).astype(jnp.bfloat16)
    return output, back_rows, hidden, back_gate, back_up


def partial_sums(row_data, grads_in, hidden, back_gate, back_up, first_slot, last_slot):
    def select(values):
        width = values.shape[-1]
        cut = values.reshape(N_DP, N_EXPERT, CAP + RCAP, width)[:, :, first_slot:last_slot]
        return cut.reshape(N_DP, N_EXPERT * (last_slot - first_slot), width).astype(jnp.float32)
    inputs_x = select(row_data)
    gate_part = jnp.einsum("knd,knf->kdf", inputs_x, select(back_gate))
    up_part = jnp.einsum("knd,knf->kdf", inputs_x, select(back_up))
    down_part = jnp.einsum("knd,knf->kdf", select(grads_in), select(hidden))
    return [lax.optimization_barrier(part.astype(jnp.bfloat16)).astype(jnp.float32) for part in (gate_part, up_part, down_part)]


def reference(tokens, cotangent, routes, route_weight, replica_pick, hot_experts, hot_holders, capacity, gate_weight, up_weight, down_weight):
    blocks = N_DP * N_EXPERT
    slot_count = CAP + RCAP
    route_count = TOK_DEV * TOPK
    total = blocks * route_count
    flat_experts = routes.reshape(blocks, route_count)
    flat_pick = replica_pick.reshape(blocks, route_count)
    route_scale = route_weight.reshape(total).astype(jnp.float32) * (1.0 / 4096.0)

    def plan_block(block_experts, block_pick):
        return plan_routes(block_experts, block_pick, hot_experts, hot_holders, capacity)

    replica, holder, kept_mask, slot_index = jax.vmap(plan_block)(flat_experts, flat_pick)
    block_ids = jnp.broadcast_to(jnp.arange(blocks, dtype=jnp.int32)[:, None], (blocks, route_count))
    route_ids = jnp.arange(total, dtype=jnp.int32).reshape(blocks, route_count)
    places = EXPERTS * blocks * slot_count
    where_to = jnp.where(kept_mask, (flat_experts * blocks + block_ids) * slot_count + slot_index, places).astype(jnp.int32)
    slot_table = jnp.full((places,), total, jnp.int32).at[where_to.reshape(total)].set(route_ids.reshape(total), mode="drop")
    slot_table = slot_table.reshape(EXPERTS, blocks * slot_count)

    def expert_step(carry, inputs):
        mixed_sum, back_sum = carry
        table_row, gate_w, up_w, down_w = inputs
        filled = table_row < total
        route_index = jnp.minimum(table_row, total - 1)
        token_index = route_index // TOPK
        row_data = jnp.where(filled[:, None], tokens[token_index], jnp.zeros((), jnp.bfloat16))
        weights = jnp.where(filled, route_scale[route_index], jnp.float32(0.0))
        grads_in = (weights[:, None] * cotangent[token_index].astype(jnp.float32)).astype(jnp.bfloat16)
        output, back_rows, hidden, back_gate, back_up = expert_rows(row_data, grads_in, gate_w, up_w, down_w)
        mixed_sum = mixed_sum.at[token_index].add(weights[:, None] * output.astype(jnp.float32))
        back_sum = back_sum.at[token_index].add(jnp.where(filled[:, None], back_rows.astype(jnp.float32), jnp.float32(0.0)))
        home = partial_sums(row_data, grads_in, hidden, back_gate, back_up, 0, CAP)
        far = partial_sums(row_data, grads_in, hidden, back_gate, back_up, CAP, slot_count)
        grads = []
        for home_part, far_part in zip(home, far):
            far_total = lax.optimization_barrier(jnp.sum(far_part, axis=0).astype(jnp.bfloat16)).astype(jnp.float32)
            grads.append((jnp.sum(home_part, axis=0) + far_total).astype(jnp.bfloat16))
        return (mixed_sum, back_sum), (grads[0], grads[1], grads[2])

    start = (jnp.zeros((TOKENS, D), jnp.float32), jnp.zeros((TOKENS, D), jnp.float32))
    (mixed_sum, back_sum), grads = lax.scan(expert_step, start, (slot_table, gate_weight, up_weight, down_weight))
    return mixed_sum.astype(jnp.bfloat16), back_sum.astype(jnp.bfloat16), grads[0], grads[1], grads[2]
```

```python
import jax
import jax.numpy as jnp
from jax import lax
from jax.experimental import pallas as pl
from jax.experimental.pallas import tpu as pltpu
from jax.sharding import PartitionSpec as P

D = 2048
FF = 768
TOPK = 8
HOT = 8
CAP = 8
RCAP = 3
TOK = 128
EXPERTS = 64
HOME = EXPERTS * CAP
FAR = EXPERTS * RCAP
PARTS = 8
PIECE = D // PARTS
WIDE = D + RCAP * PIECE
STEP = 256
BF = jnp.bfloat16
F32 = jnp.float32
VMEM_LIMIT = 56 * 1024 * 1024


def dot(a, b, dims=((1,), (0,))):
    return lax.dot_general(a, b, (dims, ((), ())), preferred_element_type=F32)


def fold_matrix(transposed):
    row = lax.broadcasted_iota(jnp.int32, (HOME, HOME), 0)
    col = lax.broadcasted_iota(jnp.int32, (HOME, HOME), 1)
    if transposed:
        row, col = col, row
    return (col == (row % EXPERTS) * PARTS + row // EXPERTS).astype(F32).astype(BF)


def unfold(folded, rows_ref):
    flat = dot(fold_matrix(False), folded).astype(BF)
    for i in range(PARTS):
        for f in range(RCAP):
            rows_ref[f * EXPERTS:(f + 1) * EXPERTS, i * PIECE:(i + 1) * PIECE] = flat[
                i * EXPERTS:(i + 1) * EXPERTS, f * PIECE:(f + 1) * PIECE
            ]


def fold(rows):
    flat = jnp.concatenate(
        [
            jnp.concatenate(
                [
                    rows[f * EXPERTS:(f + 1) * EXPERTS, i * PIECE:(i + 1) * PIECE]
                    for f in range(RCAP)
                ],
                axis=1,
            )
            for i in range(PARTS)
        ],
        axis=0,
    )
    return dot(fold_matrix(True), flat).astype(BF)


def picks(slots, scale=None):
    home_slots, far_slots = slots[:EXPERTS], slots[EXPERTS:]
    s = lax.broadcasted_iota(jnp.int32, (EXPERTS, CAP, TOK), 1).astype(F32) + 1.0
    home_value = F32(1.0) if scale is None else scale[:EXPERTS][:, None, :]
    home = jnp.where(home_slots[:, None, :] == s, home_value, 0.0).reshape(HOME, TOK)
    far_value = F32(1.0) if scale is None else scale[EXPERTS:]
    far = jnp.concatenate(
        [jnp.where(far_slots == F32(f + 1), far_value, 0.0) for f in range(RCAP)], axis=0
    )
    return home, far


def plan_kernel(hot_ref, holder_ref, cap_ref, routes_ref, weight_ref, pick_ref, tokens_ref,
                send_ref, slots_ref, scale_ref):
    lane = lax.broadcasted_iota(jnp.int32, (1, TOK), 1)
    expert = lane % EXPERTS
    far_lane = lane >= EXPERTS
    limit = jnp.zeros((1, TOK), jnp.int32)
    for e in range(EXPERTS):
        limit = jnp.where(lane == e, cap_ref[e], limit)
    hot = jnp.zeros((1, TOK), jnp.int32)
    for j in range(HOT):
        here = expert == hot_ref[j]
        hot = jnp.where(here, 1, hot)
        limit = jnp.where(
            jnp.logical_and(here, far_lane), jnp.minimum(cap_ref[holder_ref[j]], RCAP), limit
        )
    far_value = jnp.where(far_lane, 1, 0)
    present = jnp.zeros((TOK, TOK), F32)
    scale = jnp.zeros((TOK, TOK), F32)
    for k in range(TOPK):
        replica = hot * pick_ref[:, k:k + 1]
        match = jnp.logical_and(routes_ref[:, k:k + 1] == expert, replica == far_value)
        present = jnp.where(match, 1.0, present)
        scale = jnp.where(match, weight_ref[:, k:k + 1].astype(F32), scale)
    row = lax.broadcasted_iota(jnp.int32, (TOK, TOK), 0)
    col = lax.broadcasted_iota(jnp.int32, (TOK, TOK), 1)
    before = (col < row).astype(F32).astype(BF)
    same = (col == row).astype(F32).astype(BF)
    rank = dot(before, present.astype(BF))
    kept = jnp.logical_and(present > 0.0, rank < limit.astype(F32))
    slots = jnp.where(kept, rank + 1.0, 0.0).astype(BF)
    high = scale.astype(BF)
    low = (scale - high.astype(F32)).astype(BF)
    turn = ((0,), (0,))
    slots = dot(slots, same, turn)
    slots_ref[...] = slots
    scale_ref[...] = (dot(high, same, turn) + dot(low, same, turn)) * (1.0 / 4096.0)
    home, far = picks(slots)
    home, far = home.astype(BF), far.astype(BF)
    for c in range(0, D, STEP):
        send_ref[:, c:c + STEP] = dot(home, tokens_ref[:, c:c + STEP]).astype(BF)
    send_ref[:, D:] = fold(dot(far, tokens_ref[...]).astype(BF))


def split(values):
    high = values.astype(BF)
    return high, (values - high.astype(F32)).astype(BF)


def grads_kernel(slots_ref, scale_ref, cot_ref, send_ref):
    home, far = picks(slots_ref[...], scale_ref[...])
    home = jnp.concatenate(split(home), axis=1)
    far = jnp.concatenate(split(far), axis=1)
    for c in range(0, D, STEP):
        cot = cot_ref[:, c:c + STEP]
        send_ref[:, c:c + STEP] = dot(home, jnp.concatenate([cot, cot], axis=0)).astype(BF)
    cot = cot_ref[...]
    send_ref[:, D:] = fold(dot(far, jnp.concatenate([cot, cot], axis=0)).astype(BF))


def forward_kernel(got_ref, gate_ref, up_ref, down_ref,
                   send_ref, far_ref, hidden_ref, gate_factor_ref, up_factor_ref):
    unfold(got_ref[:, D:], far_ref)

    def hidden_step(n, carry):
        cols = pl.ds(pl.multiple_of(n * STEP, STEP), STEP)
        for first, rows in ((0, got_ref), (HOME, far_ref)):
            x = rows[:, :D]
            count = x.shape[0]
            pre_gate = dot(x, gate_ref[:, cols])
            pre_up = dot(x, up_ref[:, cols])
            sigma = jax.nn.sigmoid(pre_gate)
            active = pre_gate * sigma
            hidden_ref[first:first + count, cols] = (active * pre_up).astype(BF)
            gate_factor_ref[first:first + count, cols] = (
                pre_up * sigma * (1.0 + pre_gate * (1.0 - sigma))
            )
            up_factor_ref[first:first + count, cols] = active
        return carry

    lax.fori_loop(0, FF // STEP, hidden_step, 0)
    outputs(send_ref, [(hidden_ref, down_ref)])


def outputs(send_ref, pairs):
    def out_step(n, carry):
        cols = pl.ds(pl.multiple_of(n * PIECE, PIECE), PIECE)
        total = sum(dot(rows[:HOME], w[cols, :], ((1,), (1,))) for rows, w in pairs)
        send_ref[:, cols] = total.astype(BF)
        return carry

    lax.fori_loop(0, PARTS, out_step, 0)
    far = sum(dot(rows[HOME:], w[...], ((1,), (1,))) for rows, w in pairs)
    send_ref[:, D:] = fold(far.astype(BF))


def backward_kernel(got_ref, gate_ref, up_ref, down_ref, gate_factor_ref, up_factor_ref,
                    send_ref, far_ref, back_gate_ref, back_up_ref):
    unfold(got_ref[:, D:], far_ref)

    def hidden_step(n, carry):
        cols = pl.ds(pl.multiple_of(n * STEP, STEP), STEP)
        for first, rows in ((0, got_ref), (HOME, far_ref)):
            g = rows[:, :D]
            count = g.shape[0]
            back_hidden = dot(g, down_ref[:, cols])
            here = slice(first, first + count)
            back_gate_ref[here, cols] = (back_hidden * gate_factor_ref[here, cols]).astype(BF)
            back_up_ref[here, cols] = (back_hidden * up_factor_ref[here, cols]).astype(BF)
        return carry

    lax.fori_loop(0, FF // STEP, hidden_step, 0)
    outputs(send_ref, [(back_gate_ref, gate_ref), (back_up_ref, up_ref)])


def weight_kernel(home_ref, far_ref, *refs):
    count = len(refs) // 2

    def step(n, carry):
        cols = pl.ds(pl.multiple_of(n * STEP, STEP), STEP)
        home, far = home_ref[:, cols], far_ref[:, cols]
        for back, grad in zip(refs[:count], refs[count:]):
            turn = ((0,), (0,))
            grad[cols, :] = (dot(home, back[:HOME], turn) + dot(far, back[HOME:], turn)).astype(BF)
        return carry

    lax.fori_loop(0, D // STEP, step, 0)


def mixed_kernel(slots_ref, scale_ref, got_ref, mixed_ref, far_ref):
    unfold(got_ref[:, D:], far_ref)
    home, far = picks(slots_ref[...], scale_ref[...])
    home = jnp.concatenate(split(home), axis=1)
    far = jnp.concatenate(split(far), axis=1)
    turn = ((0,), (0,))
    for c in range(0, D, STEP):
        both = dot(home, got_ref[:, c:c + STEP], turn) + dot(far, far_ref[:, c:c + STEP], turn)
        mixed_ref[:, c:c + STEP] = (both[:TOK] + both[TOK:]).astype(BF)


def back_kernel(slots_ref, got_ref, grad_ref, far_ref):
    unfold(got_ref[:, D:], far_ref)
    home, far = picks(slots_ref[...])
    home, far = home.astype(BF), far.astype(BF)
    turn = ((0,), (0,))
    for c in range(0, D, STEP):
        grad_ref[:, c:c + STEP] = (
            dot(home, got_ref[:, c:c + STEP], turn) + dot(far, far_ref[:, c:c + STEP], turn)
        ).astype(BF)


def call(kernel, outs, *args, smem=0, scratch=(), flops=0):
    size = sum(a.size * a.dtype.itemsize for a in args)
    size += sum(o.size * o.dtype.itemsize for o in outs)
    vmem = pl.BlockSpec(memory_space=pltpu.VMEM)
    return pl.pallas_call(
        kernel,
        out_shape=outs,
        in_specs=[pl.BlockSpec(memory_space=pltpu.SMEM)] * smem + [vmem] * (len(args) - smem),
        out_specs=[vmem] * len(outs),
        scratch_shapes=list(scratch),
        compiler_params=pltpu.CompilerParams(vmem_limit_bytes=VMEM_LIMIT),
        cost_estimate=pl.CostEstimate(flops=flops, bytes_accessed=size, transcendentals=0),
    )(*args)


def shape(rows, cols, dtype=BF):
    return jax.ShapeDtypeStruct((rows, cols), dtype)


def exchange(values):
    return lax.all_to_all(values, "expert", split_axis=0, concat_axis=0, tiled=True)


def shards(tokens, cotangent, routes, route_weight, replica_pick, hot_experts, hot_holders,
           capacity, gate_weight, up_weight, down_weight):
    gate, up, down = gate_weight[0], up_weight[0], down_weight[0]
    rows = HOME + FAR
    product = 2 * rows * D * FF
    square = shape(TOK, TOK, F32)
    packed = shape(HOME, WIDE)
    far = shape(FAR, D)
    act, act32 = shape(rows, FF), shape(rows, FF, F32)
    far_scratch = pltpu.VMEM((FAR, D), BF)
    move = 2 * rows * TOK * D

    send_x, slots, scale = call(
        plan_kernel, [packed, square, square], hot_experts, hot_holders, capacity,
        routes, route_weight, replica_pick, tokens, smem=3, flops=move,
    )
    got_x = exchange(send_x)
    (send_g,) = call(grads_kernel, [packed], slots, scale, cotangent, flops=2 * move)
    got_g = exchange(send_g)
    send_out, far_x, hidden, gate_factor, up_factor = call(
        forward_kernel, [packed, far, act, act32, act32], got_x, gate, up, down,
        flops=3 * product,
    )
    got_out = exchange(send_out)
    send_back, far_g, back_gate, back_up = call(
        backward_kernel, [packed, far, act, act], got_g, gate, up, down, gate_factor, up_factor,
        flops=3 * product,
    )
    got_back = exchange(send_back)
    grad = shape(D, FF)
    (part_down,) = call(weight_kernel, [grad], got_g, far_g, hidden, flops=product)
    part_gate, part_up = call(
        weight_kernel, [grad, grad], got_x, far_x, back_gate, back_up, flops=2 * product
    )
    grads = [
        lax.psum_scatter(part, "dp", scatter_dimension=0, tiled=True)[None]
        for part in (part_gate, part_up, part_down)
    ]
    (mixed,) = call(
        mixed_kernel, [shape(TOK, D)], slots, scale, got_out, scratch=[far_scratch], flops=2 * move
    )
    (grad_tokens,) = call(
        back_kernel, [shape(TOK, D)], slots, got_back, scratch=[far_scratch], flops=move
    )
    return (mixed, grad_tokens, *grads)


def solution(mesh):
    tokens = P(("dp", "expert"), None)
    weights = P("expert", None, None)
    grads = P("expert", "dp", None)
    return jax.shard_map(
        shards,
        mesh=mesh,
        in_specs=(tokens,) * 5 + (P(),) * 3 + (weights,) * 3,
        out_specs=(tokens, tokens, grads, grads, grads),
        check_vma=False,
    )
```

```python
import jax
import jax.numpy as jnp
from jax import lax
from jax.experimental import pallas as pl
from jax.experimental.pallas import tpu as pltpu
from jax.sharding import PartitionSpec as P

D = 2048
FF = 768
TOPK = 8
HOT = 8
CAP = 8
RCAP = 3
TOK = 128
EXPERTS = 64
HOME = EXPERTS * CAP
FAR = EXPERTS * RCAP
PARTS = 8
PIECE = D // PARTS
HALF = D // 2
WIDE = D + RCAP * PIECE
STEP = 256
BF = jnp.bfloat16
F32 = jnp.float32
VMEM_LIMIT = 32 * 1024 * 1024


def dot(a, b, dims=((1,), (0,))):
    return lax.dot_general(a, b, (dims, ((), ())), preferred_element_type=F32)


def fold_matrix(transposed):
    row = lax.broadcasted_iota(jnp.int32, (HOME, HOME), 0)
    col = lax.broadcasted_iota(jnp.int32, (HOME, HOME), 1)
    if transposed:
        row, col = col, row
    return (col == (row % EXPERTS) * PARTS + row // EXPERTS).astype(F32).astype(BF)


def unfold(folded, rows_ref):
    flat = dot(fold_matrix(False), folded).astype(BF)
    for i in range(PARTS):
        for f in range(RCAP):
            rows_ref[f * EXPERTS:(f + 1) * EXPERTS, i * PIECE:(i + 1) * PIECE] = flat[
                i * EXPERTS:(i + 1) * EXPERTS, f * PIECE:(f + 1) * PIECE
            ]


def fold(rows):
    flat = jnp.concatenate(
        [
            jnp.concatenate(
                [
                    rows[f * EXPERTS:(f + 1) * EXPERTS, i * PIECE:(i + 1) * PIECE]
                    for f in range(RCAP)
                ],
                axis=1,
            )
            for i in range(PARTS)
        ],
        axis=0,
    )
    return dot(fold_matrix(True), flat).astype(BF)


def picks(slots, scale=None):
    home_slots, far_slots = slots[:EXPERTS], slots[EXPERTS:]
    s = lax.broadcasted_iota(jnp.int32, (EXPERTS, CAP, TOK), 1).astype(F32) + 1.0
    home_value = F32(1.0) if scale is None else scale[:EXPERTS][:, None, :]
    home = jnp.where(home_slots[:, None, :] == s, home_value, 0.0).reshape(HOME, TOK)
    far_value = F32(1.0) if scale is None else scale[EXPERTS:]
    far = jnp.concatenate(
        [jnp.where(far_slots == F32(f + 1), far_value, 0.0) for f in range(RCAP)], axis=0
    )
    return home, far


def plan_kernel(hot_ref, holder_ref, cap_ref, routes_ref, weight_ref, pick_ref, tokens_ref,
                send_ref, slots_ref, scale_ref):
    lane = lax.broadcasted_iota(jnp.int32, (1, TOK), 1)
    limit = jnp.zeros((1, TOK), jnp.int32)
    for e in range(EXPERTS):
        limit = jnp.where(lane == e, cap_ref[e], limit)
    hot = jnp.zeros((1, TOK), jnp.int32)
    for j in range(HOT):
        hot = jnp.where(lane % EXPERTS == hot_ref[j], 1, hot)
        limit = jnp.where(
            lane == EXPERTS + hot_ref[j], jnp.minimum(cap_ref[holder_ref[j]], RCAP), limit
        )
    row = lax.broadcasted_iota(jnp.int32, (TOK, TOK), 0)
    col = lax.broadcasted_iota(jnp.int32, (TOK, TOK), 1)
    limit = jnp.sum(jnp.where(row == col, limit, 0), axis=1, keepdims=True)
    hot = jnp.sum(jnp.where(row == col, hot, 0), axis=1, keepdims=True)
    expert = row % EXPERTS
    far_class = row // EXPERTS
    present = jnp.zeros((TOK, TOK), F32)
    scale = jnp.zeros((TOK, TOK), jnp.int32)
    for k in range(TOPK):
        replica = hot * pick_ref[k:k + 1, :]
        match = jnp.logical_and(routes_ref[k:k + 1, :] == expert, replica == far_class)
        present = jnp.where(match, 1.0, present)
        scale = jnp.where(match, weight_ref[k:k + 1, :], scale)
    rank = dot(present.astype(BF), (row < col).astype(F32).astype(BF))
    kept = jnp.logical_and(present > 0.0, rank < limit.astype(F32))
    slots = jnp.where(kept, rank + 1.0, 0.0)
    slots_ref[...] = slots
    scale_ref[...] = scale.astype(F32) * (1.0 / 4096.0)
    home, far = picks(slots)
    home, far = home.astype(BF), far.astype(BF)
    for c in range(0, D, STEP):
        send_ref[:, c:c + STEP] = dot(home, tokens_ref[:, c:c + STEP]).astype(BF)
    send_ref[:, D:] = fold(dot(far, tokens_ref[...]).astype(BF))


def split(values):
    high = values.astype(BF)
    return high, (values - high.astype(F32)).astype(BF)


def grads_kernel(slots_ref, scale_ref, cot_ref, send_ref):
    home, far = picks(slots_ref[...], scale_ref[...])
    home = jnp.concatenate(split(home), axis=1)
    far = jnp.concatenate(split(far), axis=1)
    for c in range(0, D, STEP):
        cot = cot_ref[:, c:c + STEP]
        send_ref[:, c:c + STEP] = dot(home, jnp.concatenate([cot, cot], axis=0)).astype(BF)
    cot = cot_ref[...]
    send_ref[:, D:] = fold(dot(far, jnp.concatenate([cot, cot], axis=0)).astype(BF))


def forward_kernel(got_ref, gate_ref, up_ref, down_ref,
                   send_ref, far_ref, hidden_ref, gate_factor_ref, up_factor_ref):
    unfold(got_ref[:, D:], far_ref)

    def hidden_step(n, carry):
        cols = pl.ds(pl.multiple_of(n * STEP, STEP), STEP)
        for first, rows in ((0, got_ref), (HOME, far_ref)):
            x = rows[:, :D]
            count = x.shape[0]
            pre_gate = dot(x, gate_ref[:, cols])
            pre_up = dot(x, up_ref[:, cols])
            sigma = jax.nn.sigmoid(pre_gate)
            active = pre_gate * sigma
            hidden_ref[first:first + count, cols] = (active * pre_up).astype(BF)
            gate_factor_ref[first:first + count, cols] = (
                pre_up * sigma * (1.0 + pre_gate * (1.0 - sigma))
            )
            up_factor_ref[first:first + count, cols] = active
        return carry

    lax.fori_loop(0, FF // STEP, hidden_step, 0)
    outputs(send_ref, [(hidden_ref, down_ref)])


def outputs(send_ref, pairs):
    def out_step(n, carry):
        cols = pl.ds(pl.multiple_of(n * PIECE, PIECE), PIECE)
        total = sum(dot(rows[:HOME], w[cols, :], ((1,), (1,))) for rows, w in pairs)
        send_ref[:, cols] = total.astype(BF)
        return carry

    lax.fori_loop(0, PARTS, out_step, 0)
    far = sum(dot(rows[HOME:], w[...], ((1,), (1,))) for rows, w in pairs)
    send_ref[:, D:] = fold(far.astype(BF))


def backward_kernel(got_ref, gate_ref, up_ref, down_ref, gate_factor_ref, up_factor_ref,
                    send_ref, far_ref, back_gate_ref, back_up_ref):
    unfold(got_ref[:, D:], far_ref)

    def hidden_step(n, carry):
        cols = pl.ds(pl.multiple_of(n * STEP, STEP), STEP)
        for first, rows in ((0, got_ref), (HOME, far_ref)):
            g = rows[:, :D]
            count = g.shape[0]
            back_hidden = dot(g, down_ref[:, cols])
            here = slice(first, first + count)
            back_gate_ref[here, cols] = (back_hidden * gate_factor_ref[here, cols]).astype(BF)
            back_up_ref[here, cols] = (back_hidden * up_factor_ref[here, cols]).astype(BF)
        return carry

    lax.fori_loop(0, FF // STEP, hidden_step, 0)
    outputs(send_ref, [(back_gate_ref, gate_ref), (back_up_ref, up_ref)])


def weight_kernel(me_ref, home_ref, far_ref, *refs):
    count = len(refs) // 3
    backs, sends, keeps = refs[:count], refs[count:2 * count], refs[2 * count:]
    turn = ((0,), (0,))
    for first, grads in (((1 - me_ref[0]) * HALF, sends), (me_ref[0] * HALF, keeps)):

        def step(n, carry, first=first, grads=grads):
            rows = pl.ds(pl.multiple_of(n * STEP, STEP), STEP)
            cols = pl.ds(pl.multiple_of(first + n * STEP, STEP), STEP)
            home, far = home_ref[:, cols], far_ref[:, cols]
            for back, grad in zip(backs, grads):
                total = dot(home, back[:HOME], turn) + dot(far, back[HOME:], turn)
                grad[rows, :] = total.astype(BF)
            return carry

        lax.fori_loop(0, HALF // STEP, step, 0)


def mixed_kernel(slots_ref, scale_ref, got_ref, mixed_ref, far_ref):
    unfold(got_ref[:, D:], far_ref)
    home, far = picks(slots_ref[...], scale_ref[...])
    home = jnp.concatenate(split(home), axis=1)
    far = jnp.concatenate(split(far), axis=1)
    turn = ((0,), (0,))
    for c in range(0, D, STEP):
        both = dot(home, got_ref[:, c:c + STEP], turn) + dot(far, far_ref[:, c:c + STEP], turn)
        mixed_ref[:, c:c + STEP] = (both[:TOK] + both[TOK:]).astype(BF)


def back_kernel(slots_ref, got_ref, grad_ref, far_ref):
    unfold(got_ref[:, D:], far_ref)
    home, far = picks(slots_ref[...])
    home, far = home.astype(BF), far.astype(BF)
    turn = ((0,), (0,))
    for c in range(0, D, STEP):
        grad_ref[:, c:c + STEP] = (
            dot(home, got_ref[:, c:c + STEP], turn) + dot(far, far_ref[:, c:c + STEP], turn)
        ).astype(BF)


def call(kernel, outs, *args, smem=0, scratch=(), flops=0):
    size = sum(a.size * a.dtype.itemsize for a in args)
    size += sum(o.size * o.dtype.itemsize for o in outs)
    vmem = pl.BlockSpec(memory_space=pltpu.VMEM)
    return pl.pallas_call(
        kernel,
        out_shape=outs,
        in_specs=[pl.BlockSpec(memory_space=pltpu.SMEM)] * smem + [vmem] * (len(args) - smem),
        out_specs=[vmem] * len(outs),
        scratch_shapes=list(scratch),
        compiler_params=pltpu.CompilerParams(vmem_limit_bytes=VMEM_LIMIT),
        cost_estimate=pl.CostEstimate(flops=flops, bytes_accessed=size, transcendentals=0),
    )(*args)


def shape(rows, cols, dtype=BF):
    return jax.ShapeDtypeStruct((rows, cols), dtype)


def exchange(values):
    return lax.all_to_all(values, "expert", split_axis=0, concat_axis=0, tiled=True)


def shards(tokens, cotangent, routes, route_weight, replica_pick, hot_experts, hot_holders,
           capacity, gate_weight, up_weight, down_weight):
    gate, up, down = gate_weight[0], up_weight[0], down_weight[0]
    rows = HOME + FAR
    product = 2 * rows * D * FF
    square = shape(TOK, TOK, F32)
    packed = shape(HOME, WIDE)
    far = shape(FAR, D)
    act, act32 = shape(rows, FF), shape(rows, FF, F32)
    far_scratch = pltpu.VMEM((FAR, D), BF)
    move = 2 * rows * TOK * D

    send_x, slots, scale = call(
        plan_kernel, [packed, square, square], hot_experts, hot_holders, capacity,
        routes.T, route_weight.T, replica_pick.T, tokens, smem=3, flops=move,
    )
    got_x = exchange(send_x)
    (send_g,) = call(grads_kernel, [packed], slots, scale, cotangent, flops=2 * move)
    got_g = exchange(send_g)
    send_out, far_x, hidden, gate_factor, up_factor = call(
        forward_kernel, [packed, far, act, act32, act32], got_x, gate, up, down,
        flops=3 * product,
    )
    got_out = exchange(send_out)
    send_back, far_g, back_gate, back_up = call(
        backward_kernel, [packed, far, act, act], got_g, gate, up, down, gate_factor, up_factor,
        flops=3 * product,
    )
    send_back, got_out = lax.optimization_barrier((send_back, got_out))
    got_back = exchange(send_back)
    half = shape(HALF, FF)
    me = lax.axis_index("dp").reshape(1)
    send_down, keep_down = call(
        weight_kernel, [half] * 2, me, got_g, far_g, hidden, smem=1, flops=product
    )
    send_gate, send_up, keep_gate, keep_up = call(
        weight_kernel, [half] * 4, me, got_x, far_x, back_gate, back_up, smem=1, flops=2 * product
    )
    grads = [
        (keep.astype(F32) + lax.ppermute(send, "dp", ((0, 1), (1, 0))).astype(F32)).astype(BF)[None]
        for send, keep in ((send_gate, keep_gate), (send_up, keep_up), (send_down, keep_down))
    ]
    (mixed,) = call(
        mixed_kernel, [shape(TOK, D)], slots, scale, got_out, scratch=[far_scratch], flops=2 * move
    )
    (grad_tokens,) = call(
        back_kernel, [shape(TOK, D)], slots, got_back, scratch=[far_scratch], flops=move
    )
    return (mixed, grad_tokens, *grads)


def solution(mesh):
    tokens = P(("dp", "expert"), None)
    weights = P("expert", None, None)
    grads = P("expert", "dp", None)
    return jax.shard_map(
        shards,
        mesh=mesh,
        in_specs=(tokens,) * 5 + (P(),) * 3 + (weights,) * 3,
        out_specs=(tokens, tokens, grads, grads, grads),
        check_vma=False,
    )
```

```python
import jax
import jax.numpy as jnp
from jax import lax
from jax.experimental import pallas as pl
from jax.experimental.pallas import tpu as pltpu
from jax.sharding import PartitionSpec as P

D = 2048
FF = 768
TOPK = 8
HOT = 8
CAP = 8
RCAP = 3
TOK = 128
EXPERTS = 64
HOME = EXPERTS * CAP
FAR = EXPERTS * RCAP
PARTS = 8
PIECE = D // PARTS
FOLD = RCAP * PIECE
WIDE = D + FOLD
ROWS = HOME + FAR
GROUP = 32
HALF = D // 2
STEP = 256
BF = jnp.bfloat16
F32 = jnp.float32
TURN = ((0,), (0,))
MIB = 1024 * 1024


def dot(a, b, dims=((1,), (0,))):
    return lax.dot_general(a, b, (dims, ((), ())), preferred_element_type=F32)


def fold_matrix(transposed=False):
    size = GROUP * PARTS
    row = lax.broadcasted_iota(jnp.int32, (size, size), 0)
    col = lax.broadcasted_iota(jnp.int32, (size, size), 1)
    if transposed:
        row, col = col, row
    return (col == (row % GROUP) * PARTS + row // GROUP).astype(F32).astype(BF)


def unfold(folded, rows_ref):
    order = fold_matrix()
    for first in range(0, EXPERTS, GROUP):
        flat = dot(order, folded[first * PARTS:(first + GROUP) * PARTS, :]).astype(BF)
        for i in range(PARTS):
            for f in range(RCAP):
                at = f * EXPERTS + first
                rows_ref[at:at + GROUP, i * PIECE:(i + 1) * PIECE] = flat[
                    i * GROUP:(i + 1) * GROUP, f * PIECE:(f + 1) * PIECE
                ]


def fold(rows, folded_ref):
    order = fold_matrix(transposed=True)
    for first in range(0, EXPERTS, GROUP):
        flat = jnp.concatenate(
            [
                jnp.concatenate(
                    [
                        rows[f * EXPERTS + first:f * EXPERTS + first + GROUP,
                             i * PIECE:(i + 1) * PIECE]
                        for f in range(RCAP)
                    ],
                    axis=1,
                )
                for i in range(PARTS)
            ],
            axis=0,
        )
        folded_ref[first * PARTS:(first + GROUP) * PARTS, :] = dot(order, flat).astype(BF)


def home_picks(slots, scale=None):
    s = lax.broadcasted_iota(jnp.int32, (EXPERTS, CAP, TOK), 1).astype(F32) + 1.0
    value = F32(1.0) if scale is None else scale[:EXPERTS][:, None, :]
    return jnp.where(slots[:EXPERTS][:, None, :] == s, value, 0.0).reshape(HOME, TOK)


def far_picks(slots, scale=None):
    value = F32(1.0) if scale is None else scale[EXPERTS:]
    return jnp.concatenate(
        [jnp.where(slots[EXPERTS:] == F32(f + 1), value, 0.0) for f in range(RCAP)], axis=0
    )


def split(values):
    high = values.astype(BF)
    return high, (values - high.astype(F32)).astype(BF)


def plan_kernel(hot_hbm, holder_hbm, cap_hbm, routes_hbm, weight_hbm, pick_hbm, tokens_hbm,
                send_hbm, slots_ref, scale_ref, hot_ref, holder_ref, cap_ref, routes_ref,
                weight_ref, pick_ref, tokens_ref, send_ref, sems, out_sems):
    copies = [
        pltpu.make_async_copy(src, dst, sems.at[i])
        for i, (src, dst) in enumerate(
            (
                (hot_hbm, hot_ref), (holder_hbm, holder_ref), (cap_hbm, cap_ref),
                (routes_hbm, routes_ref), (pick_hbm, pick_ref), (weight_hbm, weight_ref),
                (tokens_hbm, tokens_ref),
            )
        )
    ]
    for copy in copies:
        copy.start()
    for copy in copies[:-1]:
        copy.wait()
    lane = lax.broadcasted_iota(jnp.int32, (1, TOK), 1)
    limit = jnp.zeros((1, TOK), jnp.int32)
    for e in range(EXPERTS):
        limit = jnp.where(lane == e, cap_ref[e], limit)
    hot = jnp.zeros((1, TOK), jnp.int32)
    for j in range(HOT):
        hot = jnp.where(lane % EXPERTS == hot_ref[j], 1, hot)
        limit = jnp.where(
            lane == EXPERTS + hot_ref[j], jnp.minimum(cap_ref[holder_ref[j]], RCAP), limit
        )
    row = lax.broadcasted_iota(jnp.int32, (TOK, TOK), 0)
    col = lax.broadcasted_iota(jnp.int32, (TOK, TOK), 1)
    limit = jnp.sum(jnp.where(row == col, limit, 0), axis=1, keepdims=True)
    hot = jnp.sum(jnp.where(row == col, hot, 0), axis=1, keepdims=True)
    expert = row % EXPERTS
    far_class = row // EXPERTS
    present = jnp.zeros((TOK, TOK), F32)
    scale = jnp.zeros((TOK, TOK), jnp.int32)
    for k in range(TOPK):
        replica = hot * pick_ref[k:k + 1, :]
        match = jnp.logical_and(routes_ref[k:k + 1, :] == expert, replica == far_class)
        present = jnp.where(match, 1.0, present)
        scale = jnp.where(match, weight_ref[k:k + 1, :], scale)
    rank = dot(present.astype(BF), (row < col).astype(F32).astype(BF))
    kept = jnp.logical_and(present > 0.0, rank < limit.astype(F32))
    slots = jnp.where(kept, rank + 1.0, 0.0)
    slots_ref[...] = slots
    scale_ref[...] = scale.astype(F32) * (1.0 / 4096.0)
    home = home_picks(slots).astype(BF)
    copies[-1].wait()
    sends = []
    for n in range(4):
        cols = slice(n * 2 * STEP, (n + 1) * 2 * STEP)
        send_ref[:, cols] = dot(home, tokens_ref[:, cols]).astype(BF)
        sends.append(
            pltpu.make_async_copy(send_ref.at[:, cols], send_hbm.at[:, cols], out_sems.at[n])
        )
        sends[-1].start()
    fold(dot(far_picks(slots).astype(BF), tokens_ref[...]).astype(BF), send_ref.at[:, D:])
    sends.append(
        pltpu.make_async_copy(send_ref.at[:, D:], send_hbm.at[:, D:], out_sems.at[len(sends)])
    )
    sends[-1].start()
    for copy in sends:
        copy.wait()


def grads_kernel(slots_ref, scale_ref, cot_ref, send_ref, both_ref):
    slots, scale = slots_ref[...], scale_ref[...]
    both_ref[:TOK, :] = cot_ref[...]
    both_ref[TOK:, :] = cot_ref[...]
    home = jnp.concatenate(split(home_picks(slots, scale)), axis=1)
    for c in range(0, D, 2 * STEP):
        cols = slice(c, c + 2 * STEP)
        send_ref[:, cols] = dot(home, both_ref[:, cols]).astype(BF)
    far = jnp.concatenate(split(far_picks(slots, scale)), axis=1)
    fold(dot(far, both_ref[...]).astype(BF), send_ref.at[:, D:])


ACROSS = ((1,), (1,))
BLOCKS = ((HOME, FAR), (0, HOME // 2), (HOME // 2, HOME // 2))


def forward_kernel(got_ref, gate_ref, up_ref, down_ref, send_ref, far_ref, hidden_ref,
                   gate_factor_ref, up_factor_ref):
    unfold(got_ref[:, D:], far_ref)
    for first, count in BLOCKS:
        here = slice(first, first + count)
        x = far_ref[...] if first == HOME else got_ref[here, :D]
        pre_gate = dot(x, gate_ref[...])
        pre_up = dot(x, up_ref[...])
        sigma = jax.nn.sigmoid(pre_gate)
        active = pre_gate * sigma
        gate_factor_ref[here, :] = pre_up * sigma * (1.0 + pre_gate * (1.0 - sigma))
        up_factor_ref[here, :] = active
        hidden = (active * pre_up).astype(BF)
        hidden_ref[here, :] = hidden
        out = dot(hidden, down_ref[...], ACROSS).astype(BF)
        if first == HOME:
            fold(out, send_ref.at[:, D:])
        else:
            send_ref[here, :D] = out


def backward_kernel(got_ref, gate_ref, up_ref, down_ref, gate_factor_ref, up_factor_ref, send_ref,
                    far_ref, back_gate_ref, back_up_ref):
    unfold(got_ref[:, D:], far_ref)
    for first, count in BLOCKS:
        here = slice(first, first + count)
        g = far_ref[...] if first == HOME else got_ref[here, :D]
        back_hidden = dot(g, down_ref[...])
        back_gate = (back_hidden * gate_factor_ref[here, :]).astype(BF)
        back_up = (back_hidden * up_factor_ref[here, :]).astype(BF)
        back_gate_ref[here, :] = back_gate
        back_up_ref[here, :] = back_up
        back = dot(back_gate, gate_ref[...], ACROSS) + dot(back_up, up_ref[...], ACROSS)
        if first == HOME:
            fold(back.astype(BF), send_ref.at[:, D:])
        else:
            send_ref[here, :D] = back.astype(BF)


def weight_kernel(me_ref, home_ref, far_ref, *refs):
    count = len(refs) // 3
    backs, sends, keeps = refs[:count], refs[count:2 * count], refs[2 * count:]
    for half, grads in ((1 - me_ref[0], sends), (me_ref[0], keeps)):

        def step(n, carry, half=half, grads=grads):
            rows = pl.ds(pl.multiple_of(n * STEP, STEP), STEP)
            cols = pl.ds(pl.multiple_of(half * HALF + n * STEP, STEP), STEP)
            home, far = home_ref[:, cols], far_ref[:, cols]
            for back, grad in zip(backs, grads):
                total = dot(home, back[:HOME, :], TURN) + dot(far, back[HOME:, :], TURN)
                grad[rows, :] = total.astype(BF)
            return carry

        lax.fori_loop(0, HALF // STEP, step, 0)


def mixed_kernel(slots_ref, scale_ref, got_ref, mixed_ref, home_ones_ref, far_ones_ref, far_ref):
    unfold(got_ref[:, D:], far_ref)
    slots, scale = slots_ref[...], scale_ref[...]
    home = jnp.concatenate(split(home_picks(slots, scale)), axis=1)
    far = jnp.concatenate(split(far_picks(slots, scale)), axis=1)
    for c in range(0, D, STEP):
        cols = slice(c, c + STEP)
        both = dot(home, got_ref[:, cols], TURN) + dot(far, far_ref[:, cols], TURN)
        mixed_ref[:, cols] = (both[:TOK] + both[TOK:]).astype(BF)
    home_ones_ref[...] = home_picks(slots).T.astype(BF)
    far_ones_ref[...] = far_picks(slots).T.astype(BF)


def back_kernel(home_ref, far_ones_ref, got_ref, grad_ref, far_ref):
    unfold(got_ref[:, D:], far_ref)
    for c in range(0, D, 2 * STEP):
        cols = slice(c, c + 2 * STEP)
        grad_ref[:, cols] = (
            dot(home_ref[...], got_ref[:, cols]) + dot(far_ones_ref[...], far_ref[:, cols])
        ).astype(BF)


VMEM = pl.BlockSpec(memory_space=pltpu.VMEM)
SMEM = pl.BlockSpec(memory_space=pltpu.SMEM)
HBM = pl.BlockSpec(memory_space=pltpu.HBM)


def call(kernel, outs, args, flops, scratch=(), limit=32, in_specs=None, out_specs=None):
    size = sum(a.size * a.dtype.itemsize for a in args)
    size += sum(o.size * o.dtype.itemsize for o in outs)
    return pl.pallas_call(
        kernel,
        out_shape=outs,
        in_specs=in_specs or [VMEM] * len(args),
        out_specs=out_specs or [VMEM] * len(outs),
        scratch_shapes=list(scratch),
        compiler_params=pltpu.CompilerParams(vmem_limit_bytes=limit * MIB),
        cost_estimate=pl.CostEstimate(flops=flops, bytes_accessed=size, transcendentals=0),
    )(*args)


def shape(rows, cols, dtype=BF):
    return jax.ShapeDtypeStruct((rows, cols), dtype)


def exchange(values):
    return lax.all_to_all(values, "expert", split_axis=0, concat_axis=0, tiled=True)


def shards(tokens, cotangent, routes, route_weight, replica_pick, hot_experts, hot_holders,
           capacity, gate_weight, up_weight, down_weight):
    gate, up, down = gate_weight[0], up_weight[0], down_weight[0]
    product = 2 * ROWS * D * FF
    move = 2 * ROWS * TOK * D
    square = shape(TOK, TOK, F32)
    packed, far = shape(HOME, WIDE), shape(FAR, D)
    act, act32 = shape(ROWS, FF), shape(ROWS, FF, F32)
    far_scratch = pltpu.VMEM((FAR, D), BF)
    dma = pltpu.SemaphoreType.DMA

    send_x, slots, scale = call(
        plan_kernel,
        [packed, square, square],
        (hot_experts, hot_holders, capacity, routes.T, route_weight.T, replica_pick.T, tokens),
        move,
        [pltpu.SMEM((HOT,), jnp.int32), pltpu.SMEM((HOT,), jnp.int32),
         pltpu.SMEM((EXPERTS,), jnp.int32)]
        + [pltpu.VMEM((TOPK, TOK), jnp.int32)] * 3
        + [pltpu.VMEM((TOK, D), BF), pltpu.VMEM((HOME, WIDE), BF), dma((7,)), dma((5,))],
        60,
        [HBM] * 7,
        [HBM, VMEM, VMEM],
    )
    got_x = exchange(send_x)
    (send_g,) = call(
        grads_kernel, [packed], (slots, scale, cotangent), 2 * move,
        [pltpu.VMEM((2 * TOK, D), BF)],
    )
    got_g = exchange(send_g)
    send_out, far_x, hidden, gate_factor, up_factor = call(
        forward_kernel, [packed, far, act, act32, act32], (got_x, gate, up, down), 3 * product
    )
    got_out = exchange(send_out)
    send_back, far_g, back_gate, back_up = call(
        backward_kernel, [packed, far, act, act],
        (got_g, gate, up, down, gate_factor, up_factor), 3 * product,
    )
    send_back, got_out = lax.optimization_barrier((send_back, got_out))
    got_back = exchange(send_back)
    half = shape(HALF, FF)
    me = lax.axis_index("dp").reshape(1)
    send_down, keep_down = call(
        weight_kernel, [half] * 2, (me, got_g, far_g, hidden), product,
        in_specs=[SMEM] + [VMEM] * 3,
    )
    send_gate, send_up, keep_gate, keep_up = call(
        weight_kernel, [half] * 4, (me, got_x, far_x, back_gate, back_up), 2 * product,
        in_specs=[SMEM] + [VMEM] * 4,
    )
    grads = [
        (keep.astype(F32) + lax.ppermute(sent, "dp", ((0, 1), (1, 0))).astype(F32)).astype(BF)[None]
        for sent, keep in ((send_gate, keep_gate), (send_up, keep_up), (send_down, keep_down))
    ]
    mixed, home_ones, far_ones = call(
        mixed_kernel, [shape(TOK, D), shape(TOK, HOME), shape(TOK, FAR)], (slots, scale, got_out),
        2 * move, [far_scratch],
    )
    (grad_tokens,) = call(
        back_kernel, [shape(TOK, D)], (home_ones, far_ones, got_back), move, [far_scratch]
    )
    return (mixed, grad_tokens, *grads)


def solution(mesh):
    tokens = P(("dp", "expert"), None)
    weights = P("expert", None, None)
    grads = P("expert", "dp", None)
    return jax.shard_map(
        shards,
        mesh=mesh,
        in_specs=(tokens,) * 5 + (P(),) * 3 + (weights,) * 3,
        out_specs=(tokens, tokens, grads, grads, grads),
        check_vma=False,
    )
```

```python
import jax
import jax.numpy as jnp
from jax import lax
from jax.experimental import pallas as pl
from jax.experimental.pallas import tpu as pltpu
from jax.sharding import PartitionSpec as P

D = 2048
FF = 768
TOPK = 8
HOT = 8
CAP = 8
RCAP = 3
TOK = 128
EXPERTS = 64
HOME = EXPERTS * CAP
FAR = EXPERTS * RCAP
PARTS = 8
PIECE = D // PARTS
FOLD = RCAP * PIECE
WIDE = D + FOLD
ROWS = HOME + FAR
GROUP = 32
HALF = D // 2
STEP = 256
LATER = 750
BF = jnp.bfloat16
F32 = jnp.float32
TURN = ((0,), (0,))
MIB = 1024 * 1024


def dot(a, b, dims=((1,), (0,))):
    return lax.dot_general(a, b, (dims, ((), ())), preferred_element_type=F32)


def fold_matrix(transposed=False):
    size = GROUP * PARTS
    row = lax.broadcasted_iota(jnp.int32, (size, size), 0)
    col = lax.broadcasted_iota(jnp.int32, (size, size), 1)
    if transposed:
        row, col = col, row
    return (col == (row % GROUP) * PARTS + row // GROUP).astype(F32).astype(BF)


def unfold(folded, rows_ref):
    order = fold_matrix()
    for first in range(0, EXPERTS, GROUP):
        flat = dot(order, folded[first * PARTS:(first + GROUP) * PARTS, :]).astype(BF)
        for i in range(PARTS):
            for f in range(RCAP):
                at = f * EXPERTS + first
                rows_ref[at:at + GROUP, i * PIECE:(i + 1) * PIECE] = flat[
                    i * GROUP:(i + 1) * GROUP, f * PIECE:(f + 1) * PIECE
                ]


def fold(rows, folded_ref):
    order = fold_matrix(transposed=True)
    for first in range(0, EXPERTS, GROUP):
        flat = jnp.concatenate(
            [
                jnp.concatenate(
                    [
                        rows[f * EXPERTS + first:f * EXPERTS + first + GROUP,
                             i * PIECE:(i + 1) * PIECE]
                        for f in range(RCAP)
                    ],
                    axis=1,
                )
                for i in range(PARTS)
            ],
            axis=0,
        )
        folded_ref[first * PARTS:(first + GROUP) * PARTS, :] = dot(order, flat).astype(BF)


def home_picks(slots, scale=None):
    s = lax.broadcasted_iota(jnp.int32, (EXPERTS, CAP, TOK), 1).astype(F32) + 1.0
    value = F32(1.0) if scale is None else scale[:EXPERTS][:, None, :]
    return jnp.where(slots[:EXPERTS][:, None, :] == s, value, 0.0).reshape(HOME, TOK)


def far_picks(slots, scale=None):
    value = F32(1.0) if scale is None else scale[EXPERTS:]
    return jnp.concatenate(
        [jnp.where(slots[EXPERTS:] == F32(f + 1), value, 0.0) for f in range(RCAP)], axis=0
    )


def split(values):
    high = values.astype(BF)
    return high, (values - high.astype(F32)).astype(BF)


def plan_kernel(me_ref, hot_hbm, holder_hbm, cap_hbm, routes_hbm, weight_hbm, pick_hbm, tokens_hbm,
                send_hbm, slots_ref, scale_ref, hot_ref, holder_ref, cap_ref, routes_ref,
                weight_ref, pick_ref, tokens_ref, send_ref, later_ref, sems, out_sems):
    copies = [
        pltpu.make_async_copy(src, dst, sems.at[i])
        for i, (src, dst) in enumerate(
            (
                (hot_hbm, hot_ref), (holder_hbm, holder_ref), (cap_hbm, cap_ref),
                (routes_hbm, routes_ref), (pick_hbm, pick_ref), (weight_hbm, weight_ref),
                (tokens_hbm, tokens_ref),
            )
        )
    ]
    for copy in copies:
        copy.start()
    later_ref[...] = jnp.ones(later_ref.shape, F32)

    def turn(step, carry):
        value = later_ref[...]
        for _ in range(8):
            value = value * 0.5 + 1.0
        later_ref[...] = value
        return carry

    lax.fori_loop(0, me_ref[0] * LATER, turn, 0)
    for copy in copies[:-1]:
        copy.wait()
    lane = lax.broadcasted_iota(jnp.int32, (1, TOK), 1)
    limit = jnp.zeros((1, TOK), jnp.int32)
    for e in range(EXPERTS):
        limit = jnp.where(lane == e, cap_ref[e], limit)
    hot = jnp.zeros((1, TOK), jnp.int32)
    for j in range(HOT):
        hot = jnp.where(lane % EXPERTS == hot_ref[j], 1, hot)
        limit = jnp.where(
            lane == EXPERTS + hot_ref[j], jnp.minimum(cap_ref[holder_ref[j]], RCAP), limit
        )
    row = lax.broadcasted_iota(jnp.int32, (TOK, TOK), 0)
    col = lax.broadcasted_iota(jnp.int32, (TOK, TOK), 1)
    limit = jnp.sum(jnp.where(row == col, limit, 0), axis=1, keepdims=True)
    hot = jnp.sum(jnp.where(row == col, hot, 0), axis=1, keepdims=True)
    expert = row % EXPERTS
    far_class = row // EXPERTS
    present = jnp.zeros((TOK, TOK), F32)
    scale = jnp.zeros((TOK, TOK), jnp.int32)
    for k in range(TOPK):
        replica = hot * pick_ref[k:k + 1, :]
        match = jnp.logical_and(routes_ref[k:k + 1, :] == expert, replica == far_class)
        present = jnp.where(match, 1.0, present)
        scale = jnp.where(match, weight_ref[k:k + 1, :], scale)
    rank = dot(present.astype(BF), (row < col).astype(F32).astype(BF))
    kept = jnp.logical_and(present > 0.0, rank < limit.astype(F32))
    slots = jnp.where(kept, rank + 1.0, 0.0)
    slots_ref[...] = slots
    scale_ref[...] = scale.astype(F32) * (1.0 / 4096.0)
    home = home_picks(slots).astype(BF)
    copies[-1].wait()
    sends = []
    for n in range(4):
        cols = slice(n * 2 * STEP, (n + 1) * 2 * STEP)
        send_ref[:, cols] = dot(home, tokens_ref[:, cols]).astype(BF)
        sends.append(
            pltpu.make_async_copy(send_ref.at[:, cols], send_hbm.at[:, cols], out_sems.at[n])
        )
        sends[-1].start()
    fold(dot(far_picks(slots).astype(BF), tokens_ref[...]).astype(BF), send_ref.at[:, D:])
    sends.append(
        pltpu.make_async_copy(send_ref.at[:, D:], send_hbm.at[:, D:], out_sems.at[len(sends)])
    )
    sends[-1].start()
    for copy in sends:
        copy.wait()


def grads_kernel(slots_ref, scale_ref, cot_ref, send_ref, both_ref):
    slots, scale = slots_ref[...], scale_ref[...]
    both_ref[:TOK, :] = cot_ref[...]
    both_ref[TOK:, :] = cot_ref[...]
    home = jnp.concatenate(split(home_picks(slots, scale)), axis=1)
    for c in range(0, D, 2 * STEP):
        cols = slice(c, c + 2 * STEP)
        send_ref[:, cols] = dot(home, both_ref[:, cols]).astype(BF)
    far = jnp.concatenate(split(far_picks(slots, scale)), axis=1)
    fold(dot(far, both_ref[...]).astype(BF), send_ref.at[:, D:])


ACROSS = ((1,), (1,))
BLOCKS = ((HOME, FAR), (0, HOME // 2), (HOME // 2, HOME // 2))


def forward_kernel(got_ref, gate_ref, up_ref, down_ref, send_ref, far_ref, hidden_ref,
                   gate_factor_ref, up_factor_ref):
    unfold(got_ref[:, D:], far_ref)
    for first, count in BLOCKS:
        here = slice(first, first + count)
        x = far_ref[...] if first == HOME else got_ref[here, :D]
        pre_gate = dot(x, gate_ref[...])
        pre_up = dot(x, up_ref[...])
        sigma = jax.nn.sigmoid(pre_gate)
        active = pre_gate * sigma
        gate_factor_ref[here, :] = pre_up * sigma * (1.0 + pre_gate * (1.0 - sigma))
        up_factor_ref[here, :] = active
        hidden = (active * pre_up).astype(BF)
        hidden_ref[here, :] = hidden
        out = dot(hidden, down_ref[...], ACROSS).astype(BF)
        if first == HOME:
            fold(out, send_ref.at[:, D:])
        else:
            send_ref[here, :D] = out


def backward_kernel(got_ref, gate_ref, up_ref, down_ref, gate_factor_ref, up_factor_ref, send_ref,
                    far_ref, back_gate_ref, back_up_ref):
    unfold(got_ref[:, D:], far_ref)
    for first, count in BLOCKS:
        here = slice(first, first + count)
        g = far_ref[...] if first == HOME else got_ref[here, :D]
        back_hidden = dot(g, down_ref[...])
        back_gate = (back_hidden * gate_factor_ref[here, :]).astype(BF)
        back_up = (back_hidden * up_factor_ref[here, :]).astype(BF)
        back_gate_ref[here, :] = back_gate
        back_up_ref[here, :] = back_up
        back = dot(back_gate, gate_ref[...], ACROSS) + dot(back_up, up_ref[...], ACROSS)
        if first == HOME:
            fold(back.astype(BF), send_ref.at[:, D:])
        else:
            send_ref[here, :D] = back.astype(BF)


def weight_kernel(me_ref, home_ref, far_ref, *refs):
    count = len(refs) // 3
    backs, sends, keeps = refs[:count], refs[count:2 * count], refs[2 * count:]
    for half, grads in ((1 - me_ref[0], sends), (me_ref[0], keeps)):

        def step(n, carry, half=half, grads=grads):
            rows = pl.ds(pl.multiple_of(n * STEP, STEP), STEP)
            cols = pl.ds(pl.multiple_of(half * HALF + n * STEP, STEP), STEP)
            home, far = home_ref[:, cols], far_ref[:, cols]
            for back, grad in zip(backs, grads):
                total = dot(home, back[:HOME, :], TURN) + dot(far, back[HOME:, :], TURN)
                grad[rows, :] = total.astype(BF)
            return carry

        lax.fori_loop(0, HALF // STEP, step, 0)


def mixed_kernel(slots_ref, scale_ref, got_ref, mixed_ref, home_ones_ref, far_ones_ref, far_ref):
    unfold(got_ref[:, D:], far_ref)
    slots, scale = slots_ref[...], scale_ref[...]
    home = jnp.concatenate(split(home_picks(slots, scale)), axis=1)
    far = jnp.concatenate(split(far_picks(slots, scale)), axis=1)
    for c in range(0, D, STEP):
        cols = slice(c, c + STEP)
        both = dot(home, got_ref[:, cols], TURN) + dot(far, far_ref[:, cols], TURN)
        mixed_ref[:, cols] = (both[:TOK] + both[TOK:]).astype(BF)
    home_ones_ref[...] = home_picks(slots).T.astype(BF)
    far_ones_ref[...] = far_picks(slots).T.astype(BF)


def back_kernel(home_ref, far_ones_ref, got_ref, grad_ref, far_ref):
    unfold(got_ref[:, D:], far_ref)
    for c in range(0, D, 2 * STEP):
        cols = slice(c, c + 2 * STEP)
        grad_ref[:, cols] = (
            dot(home_ref[...], got_ref[:, cols]) + dot(far_ones_ref[...], far_ref[:, cols])
        ).astype(BF)


VMEM = pl.BlockSpec(memory_space=pltpu.VMEM)
SMEM = pl.BlockSpec(memory_space=pltpu.SMEM)
HBM = pl.BlockSpec(memory_space=pltpu.HBM)


def call(kernel, outs, args, flops, scratch=(), limit=32, in_specs=None, out_specs=None):
    size = sum(a.size * a.dtype.itemsize for a in args)
    size += sum(o.size * o.dtype.itemsize for o in outs)
    return pl.pallas_call(
        kernel,
        out_shape=outs,
        in_specs=in_specs or [VMEM] * len(args),
        out_specs=out_specs or [VMEM] * len(outs),
        scratch_shapes=list(scratch),
        compiler_params=pltpu.CompilerParams(vmem_limit_bytes=limit * MIB),
        cost_estimate=pl.CostEstimate(flops=flops, bytes_accessed=size, transcendentals=0),
    )(*args)


def shape(rows, cols, dtype=BF):
    return jax.ShapeDtypeStruct((rows, cols), dtype)


def exchange(values):
    return lax.all_to_all(values, "expert", split_axis=0, concat_axis=0, tiled=True)


def shards(tokens, cotangent, routes, route_weight, replica_pick, hot_experts, hot_holders,
           capacity, gate_weight, up_weight, down_weight):
    gate, up, down = gate_weight[0], up_weight[0], down_weight[0]
    product = 2 * ROWS * D * FF
    move = 2 * ROWS * TOK * D
    square = shape(TOK, TOK, F32)
    packed, far = shape(HOME, WIDE), shape(FAR, D)
    act, act32 = shape(ROWS, FF), shape(ROWS, FF, F32)
    far_scratch = pltpu.VMEM((FAR, D), BF)
    dma = pltpu.SemaphoreType.DMA

    me = lax.axis_index("dp").reshape(1)
    send_x, slots, scale = call(
        plan_kernel,
        [packed, square, square],
        (me, hot_experts, hot_holders, capacity, routes.T, route_weight.T, replica_pick.T, tokens),
        move,
        [pltpu.SMEM((HOT,), jnp.int32), pltpu.SMEM((HOT,), jnp.int32),
         pltpu.SMEM((EXPERTS,), jnp.int32)]
        + [pltpu.VMEM((TOPK, TOK), jnp.int32)] * 3
        + [pltpu.VMEM((TOK, D), BF), pltpu.VMEM((HOME, WIDE), BF), pltpu.VMEM((8, TOK), F32), dma((7,)), dma((5,))],
        60,
        [SMEM] + [HBM] * 7,
        [HBM, VMEM, VMEM],
    )
    got_x = exchange(send_x)
    (send_g,) = call(
        grads_kernel, [packed], (slots, scale, cotangent), 2 * move,
        [pltpu.VMEM((2 * TOK, D), BF)],
    )
    got_g = exchange(send_g)
    send_out, far_x, hidden, gate_factor, up_factor = call(
        forward_kernel, [packed, far, act, act32, act32], (got_x, gate, up, down), 3 * product
    )
    got_out = exchange(send_out)
    send_back, far_g, back_gate, back_up = call(
        backward_kernel, [packed, far, act, act],
        (got_g, gate, up, down, gate_factor, up_factor), 3 * product,
    )
    send_back, got_out = lax.optimization_barrier((send_back, got_out))
    got_back = exchange(send_back)
    half = shape(HALF, FF)
    send_down, keep_down = call(
        weight_kernel, [half] * 2, (me, got_g, far_g, hidden), product,
        in_specs=[SMEM] + [VMEM] * 3,
    )
    send_gate, send_up, keep_gate, keep_up = call(
        weight_kernel, [half] * 4, (me, got_x, far_x, back_gate, back_up), 2 * product,
        in_specs=[SMEM] + [VMEM] * 4,
    )
    grads = [
        (keep.astype(F32) + lax.ppermute(sent, "dp", ((0, 1), (1, 0))).astype(F32)).astype(BF)[None]
        for sent, keep in ((send_gate, keep_gate), (send_up, keep_up), (send_down, keep_down))
    ]
    mixed, home_ones, far_ones = call(
        mixed_kernel, [shape(TOK, D), shape(TOK, HOME), shape(TOK, FAR)], (slots, scale, got_out),
        2 * move, [far_scratch],
    )
    (grad_tokens,) = call(
        back_kernel, [shape(TOK, D)], (home_ones, far_ones, got_back), move, [far_scratch]
    )
    return (mixed, grad_tokens, *grads)


def solution(mesh):
    tokens = P(("dp", "expert"), None)
    weights = P("expert", None, None)
    grads = P("expert", "dp", None)
    return jax.shard_map(
        shards,
        mesh=mesh,
        in_specs=(tokens,) * 5 + (P(),) * 3 + (weights,) * 3,
        out_specs=(tokens, tokens, grads, grads, grads),
        check_vma=False,
    )
```

```python
import jax
import jax.numpy as jnp
from jax import lax
from jax.experimental import pallas as pl
from jax.experimental.pallas import tpu as pltpu
from jax.sharding import PartitionSpec as P

D = 2048
FF = 768
TOPK = 8
HOT = 8
CAP = 8
RCAP = 3
TOK = 128
EXPERTS = 64
HOME = EXPERTS * CAP
FAR = EXPERTS * RCAP
PARTS = 8
PIECE = D // PARTS
FOLD = RCAP * PIECE
WIDE = D + FOLD
ROWS = HOME + FAR
GROUP = 32
HALF = D // 2
STEP = 256
LATER = 810
BF = jnp.bfloat16
F32 = jnp.float32
TURN = ((0,), (0,))
MIB = 1024 * 1024


def dot(a, b, dims=((1,), (0,))):
    return lax.dot_general(a, b, (dims, ((), ())), preferred_element_type=F32)


def fold_matrix(transposed=False):
    size = GROUP * PARTS
    row = lax.broadcasted_iota(jnp.int32, (size, size), 0)
    col = lax.broadcasted_iota(jnp.int32, (size, size), 1)
    if transposed:
        row, col = col, row
    return (col == (row % GROUP) * PARTS + row // GROUP).astype(F32).astype(BF)


def unfold(folded, rows_ref):
    order = fold_matrix()
    for first in range(0, EXPERTS, GROUP):
        flat = dot(order, folded[first * PARTS:(first + GROUP) * PARTS, :]).astype(BF)
        for i in range(PARTS):
            for f in range(RCAP):
                at = f * EXPERTS + first
                rows_ref[at:at + GROUP, i * PIECE:(i + 1) * PIECE] = flat[
                    i * GROUP:(i + 1) * GROUP, f * PIECE:(f + 1) * PIECE
                ]


def fold(rows, folded_ref):
    order = fold_matrix(transposed=True)
    for first in range(0, EXPERTS, GROUP):
        flat = jnp.concatenate(
            [
                jnp.concatenate(
                    [
                        rows[f * EXPERTS + first:f * EXPERTS + first + GROUP,
                             i * PIECE:(i + 1) * PIECE]
                        for f in range(RCAP)
                    ],
                    axis=1,
                )
                for i in range(PARTS)
            ],
            axis=0,
        )
        folded_ref[first * PARTS:(first + GROUP) * PARTS, :] = dot(order, flat).astype(BF)


def home_picks(slots, scale=None):
    s = lax.broadcasted_iota(jnp.int32, (EXPERTS, CAP, TOK), 1).astype(F32) + 1.0
    value = F32(1.0) if scale is None else scale[:EXPERTS][:, None, :]
    return jnp.where(slots[:EXPERTS][:, None, :] == s, value, 0.0).reshape(HOME, TOK)


def far_picks(slots, scale=None):
    value = F32(1.0) if scale is None else scale[EXPERTS:]
    return jnp.concatenate(
        [jnp.where(slots[EXPERTS:] == F32(f + 1), value, 0.0) for f in range(RCAP)], axis=0
    )


def split(values):
    high = values.astype(BF)
    return high, (values - high.astype(F32)).astype(BF)


def plan_kernel(me_ref, hot_hbm, holder_hbm, cap_hbm, routes_hbm, weight_hbm, pick_hbm, tokens_hbm,
                send_hbm, slots_ref, scale_ref, hot_ref, holder_ref, cap_ref, routes_ref,
                weight_ref, pick_ref, tokens_ref, send_ref, later_ref, sems, out_sems):
    copies = [
        pltpu.make_async_copy(src, dst, sems.at[i])
        for i, (src, dst) in enumerate(
            (
                (hot_hbm, hot_ref), (holder_hbm, holder_ref), (cap_hbm, cap_ref),
                (routes_hbm, routes_ref), (pick_hbm, pick_ref), (weight_hbm, weight_ref),
                (tokens_hbm, tokens_ref),
            )
        )
    ]
    for copy in copies:
        copy.start()
    later_ref[...] = jnp.ones(later_ref.shape, F32)

    def turn(step, carry):
        value = later_ref[...]
        for _ in range(8):
            value = value * 0.5 + 1.0
        later_ref[...] = value
        return carry

    lax.fori_loop(0, me_ref[0] * LATER, turn, 0)
    for copy in copies[:-1]:
        copy.wait()
    lane = lax.broadcasted_iota(jnp.int32, (1, TOK), 1)
    limit = jnp.zeros((1, TOK), jnp.int32)
    for e in range(EXPERTS):
        limit = jnp.where(lane == e, cap_ref[e], limit)
    hot = jnp.zeros((1, TOK), jnp.int32)
    for j in range(HOT):
        hot = jnp.where(lane % EXPERTS == hot_ref[j], 1, hot)
        limit = jnp.where(
            lane == EXPERTS + hot_ref[j], jnp.minimum(cap_ref[holder_ref[j]], RCAP), limit
        )
    row = lax.broadcasted_iota(jnp.int32, (TOK, TOK), 0)
    col = lax.broadcasted_iota(jnp.int32, (TOK, TOK), 1)
    limit = jnp.sum(jnp.where(row == col, limit, 0), axis=1, keepdims=True)
    hot = jnp.sum(jnp.where(row == col, hot, 0), axis=1, keepdims=True)
    expert = row % EXPERTS
    far_class = row // EXPERTS
    present = jnp.zeros((TOK, TOK), F32)
    scale = jnp.zeros((TOK, TOK), jnp.int32)
    for k in range(TOPK):
        replica = hot * pick_ref[k:k + 1, :]
        match = jnp.logical_and(routes_ref[k:k + 1, :] == expert, replica == far_class)
        present = jnp.where(match, 1.0, present)
        scale = jnp.where(match, weight_ref[k:k + 1, :], scale)
    rank = dot(present.astype(BF), (row < col).astype(F32).astype(BF))
    kept = jnp.logical_and(present > 0.0, rank < limit.astype(F32))
    slots = jnp.where(kept, rank + 1.0, 0.0)
    slots_ref[...] = slots
    scale_ref[...] = scale.astype(F32) * (1.0 / 4096.0)
    home = home_picks(slots).astype(BF)
    copies[-1].wait()
    sends = []
    for n in range(4):
        cols = slice(n * 2 * STEP, (n + 1) * 2 * STEP)
        send_ref[:, cols] = dot(home, tokens_ref[:, cols]).astype(BF)
        sends.append(
            pltpu.make_async_copy(send_ref.at[:, cols], send_hbm.at[:, cols], out_sems.at[n])
        )
        sends[-1].start()
    fold(dot(far_picks(slots).astype(BF), tokens_ref[...]).astype(BF), send_ref.at[:, D:])
    sends.append(
        pltpu.make_async_copy(send_ref.at[:, D:], send_hbm.at[:, D:], out_sems.at[len(sends)])
    )
    sends[-1].start()
    for copy in sends:
        copy.wait()


def grads_kernel(slots_ref, scale_ref, cot_ref, send_ref, both_ref):
    slots, scale = slots_ref[...], scale_ref[...]
    both_ref[:TOK, :] = cot_ref[...]
    both_ref[TOK:, :] = cot_ref[...]
    home = jnp.concatenate(split(home_picks(slots, scale)), axis=1)
    for c in range(0, D, 2 * STEP):
        cols = slice(c, c + 2 * STEP)
        send_ref[:, cols] = dot(home, both_ref[:, cols]).astype(BF)
    far = jnp.concatenate(split(far_picks(slots, scale)), axis=1)
    fold(dot(far, both_ref[...]).astype(BF), send_ref.at[:, D:])


ACROSS = ((1,), (1,))
BLOCKS = ((HOME, FAR), (0, HOME // 2), (HOME // 2, HOME // 2))


def forward_kernel(got_ref, gate_ref, up_ref, down_ref, send_ref, far_ref, hidden_ref,
                   gate_factor_ref, up_factor_ref):
    unfold(got_ref[:, D:], far_ref)
    for first, count in BLOCKS:
        here = slice(first, first + count)
        x = far_ref[...] if first == HOME else got_ref[here, :D]
        pre_gate = dot(x, gate_ref[...])
        pre_up = dot(x, up_ref[...])
        sigma = jax.nn.sigmoid(pre_gate)
        active = pre_gate * sigma
        gate_factor_ref[here, :] = pre_up * sigma * (1.0 + pre_gate * (1.0 - sigma))
        up_factor_ref[here, :] = active
        hidden = (active * pre_up).astype(BF)
        hidden_ref[here, :] = hidden
        out = dot(hidden, down_ref[...], ACROSS).astype(BF)
        if first == HOME:
            fold(out, send_ref.at[:, D:])
        else:
            send_ref[here, :D] = out


def backward_kernel(got_ref, gate_ref, up_ref, down_ref, gate_factor_ref, up_factor_ref, send_ref,
                    far_ref, back_gate_ref, back_up_ref):
    unfold(got_ref[:, D:], far_ref)
    for first, count in BLOCKS:
        here = slice(first, first + count)
        g = far_ref[...] if first == HOME else got_ref[here, :D]
        back_hidden = dot(g, down_ref[...])
        back_gate = (back_hidden * gate_factor_ref[here, :]).astype(BF)
        back_up = (back_hidden * up_factor_ref[here, :]).astype(BF)
        back_gate_ref[here, :] = back_gate
        back_up_ref[here, :] = back_up
        back = dot(back_gate, gate_ref[...], ACROSS) + dot(back_up, up_ref[...], ACROSS)
        if first == HOME:
            fold(back.astype(BF), send_ref.at[:, D:])
        else:
            send_ref[here, :D] = back.astype(BF)


def weight_kernel(me_ref, home_ref, far_ref, *refs):
    count = len(refs) // 3
    backs, sends, keeps = refs[:count], refs[count:2 * count], refs[2 * count:]
    for half, grads in ((1 - me_ref[0], sends), (me_ref[0], keeps)):

        def step(n, carry, half=half, grads=grads):
            rows = pl.ds(pl.multiple_of(n * STEP, STEP), STEP)
            cols = pl.ds(pl.multiple_of(half * HALF + n * STEP, STEP), STEP)
            home, far = home_ref[:, cols], far_ref[:, cols]
            for back, grad in zip(backs, grads):
                total = dot(home, back[:HOME, :], TURN) + dot(far, back[HOME:, :], TURN)
                grad[rows, :] = total.astype(BF)
            return carry

        lax.fori_loop(0, HALF // STEP, step, 0)


def mixed_kernel(slots_ref, scale_ref, got_ref, mixed_ref, home_ones_ref, far_ones_ref, far_ref):
    unfold(got_ref[:, D:], far_ref)
    slots, scale = slots_ref[...], scale_ref[...]
    home = jnp.concatenate(split(home_picks(slots, scale)), axis=1)
    far = jnp.concatenate(split(far_picks(slots, scale)), axis=1)
    for c in range(0, D, STEP):
        cols = slice(c, c + STEP)
        both = dot(home, got_ref[:, cols], TURN) + dot(far, far_ref[:, cols], TURN)
        mixed_ref[:, cols] = (both[:TOK] + both[TOK:]).astype(BF)
    home_ones_ref[...] = home_picks(slots).T.astype(BF)
    far_ones_ref[...] = far_picks(slots).T.astype(BF)


def back_kernel(home_ref, far_ones_ref, got_ref, grad_ref, far_ref):
    unfold(got_ref[:, D:], far_ref)
    for c in range(0, D, 2 * STEP):
        cols = slice(c, c + 2 * STEP)
        grad_ref[:, cols] = (
            dot(home_ref[...], got_ref[:, cols]) + dot(far_ones_ref[...], far_ref[:, cols])
        ).astype(BF)


VMEM = pl.BlockSpec(memory_space=pltpu.VMEM)
SMEM = pl.BlockSpec(memory_space=pltpu.SMEM)
HBM = pl.BlockSpec(memory_space=pltpu.HBM)


def call(kernel, outs, args, flops, scratch=(), limit=32, in_specs=None, out_specs=None):
    size = sum(a.size * a.dtype.itemsize for a in args)
    size += sum(o.size * o.dtype.itemsize for o in outs)
    return pl.pallas_call(
        kernel,
        out_shape=outs,
        in_specs=in_specs or [VMEM] * len(args),
        out_specs=out_specs or [VMEM] * len(outs),
        scratch_shapes=list(scratch),
        compiler_params=pltpu.CompilerParams(vmem_limit_bytes=limit * MIB),
        cost_estimate=pl.CostEstimate(flops=flops, bytes_accessed=size, transcendentals=0),
    )(*args)


def shape(rows, cols, dtype=BF):
    return jax.ShapeDtypeStruct((rows, cols), dtype)


def exchange(values):
    return lax.all_to_all(values, "expert", split_axis=0, concat_axis=0, tiled=True)


def shards(tokens, cotangent, routes, route_weight, replica_pick, hot_experts, hot_holders,
           capacity, gate_weight, up_weight, down_weight):
    gate, up, down = gate_weight[0], up_weight[0], down_weight[0]
    product = 2 * ROWS * D * FF
    move = 2 * ROWS * TOK * D
    square = shape(TOK, TOK, F32)
    packed, far = shape(HOME, WIDE), shape(FAR, D)
    act, act32 = shape(ROWS, FF), shape(ROWS, FF, F32)
    far_scratch = pltpu.VMEM((FAR, D), BF)
    dma = pltpu.SemaphoreType.DMA

    me = lax.axis_index("dp").reshape(1)
    send_x, slots, scale = call(
        plan_kernel,
        [packed, square, square],
        (me, hot_experts, hot_holders, capacity, routes.T, route_weight.T, replica_pick.T, tokens),
        move,
        [pltpu.SMEM((HOT,), jnp.int32), pltpu.SMEM((HOT,), jnp.int32),
         pltpu.SMEM((EXPERTS,), jnp.int32)]
        + [pltpu.VMEM((TOPK, TOK), jnp.int32)] * 3
        + [pltpu.VMEM((TOK, D), BF), pltpu.VMEM((HOME, WIDE), BF), pltpu.VMEM((8, TOK), F32), dma((7,)), dma((5,))],
        60,
        [SMEM] + [HBM] * 7,
        [HBM, VMEM, VMEM],
    )
    got_x = exchange(send_x)
    cotangent, got_x = lax.optimization_barrier((cotangent, got_x))
    (send_g,) = call(
        grads_kernel, [packed], (slots, scale, cotangent), 2 * move,
        [pltpu.VMEM((2 * TOK, D), BF)],
    )
    got_g = exchange(send_g)
    send_out, far_x, hidden, gate_factor, up_factor = call(
        forward_kernel, [packed, far, act, act32, act32], (got_x, gate, up, down), 3 * product
    )
    got_out = exchange(send_out)
    send_back, far_g, back_gate, back_up = call(
        backward_kernel, [packed, far, act, act],
        (got_g, gate, up, down, gate_factor, up_factor), 3 * product,
    )
    send_back, got_out = lax.optimization_barrier((send_back, got_out))
    got_back = exchange(send_back)
    half = shape(HALF, FF)
    send_down, keep_down = call(
        weight_kernel, [half] * 2, (me, got_g, far_g, hidden), product, limit=20,
        in_specs=[SMEM] + [VMEM] * 3,
    )
    send_gate, send_up, keep_gate, keep_up = call(
        weight_kernel, [half] * 4, (me, got_x, far_x, back_gate, back_up), 2 * product,
        limit=20,
        in_specs=[SMEM] + [VMEM] * 4,
    )
    grads = [
        (keep.astype(F32) + lax.ppermute(sent, "dp", ((0, 1), (1, 0))).astype(F32)).astype(BF)[None]
        for sent, keep in ((send_gate, keep_gate), (send_up, keep_up), (send_down, keep_down))
    ]
    mixed, home_ones, far_ones = call(
        mixed_kernel, [shape(TOK, D), shape(TOK, HOME), shape(TOK, FAR)], (slots, scale, got_out),
        2 * move, [far_scratch], 16,
    )
    (grad_tokens,) = call(
        back_kernel, [shape(TOK, D)], (home_ones, far_ones, got_back), move, [far_scratch], 16
    )
    return (mixed, grad_tokens, *grads)


def solution(mesh):
    tokens = P(("dp", "expert"), None)
    weights = P("expert", None, None)
    grads = P("expert", "dp", None)
    return jax.shard_map(
        shards,
        mesh=mesh,
        in_specs=(tokens,) * 5 + (P(),) * 3 + (weights,) * 3,
        out_specs=(tokens, tokens, grads, grads, grads),
        check_vma=False,
    )
```

```python
import jax
import jax.numpy as jnp
from jax import lax
from jax.experimental import pallas as pl
from jax.experimental.pallas import tpu as pltpu
from jax.sharding import PartitionSpec as P

D = 2048
FF = 768
TOPK = 8
HOT = 8
CAP = 8
RCAP = 3
TOK = 128
EXPERTS = 64
HOME = EXPERTS * CAP
FAR = EXPERTS * RCAP
PARTS = 8
PIECE = D // PARTS
FOLD = RCAP * PIECE
WIDE = D + FOLD
ROWS = HOME + FAR
GROUP = 32
HALF = D // 2
STEP = 256
LATER = 820
BF = jnp.bfloat16
F32 = jnp.float32
TURN = ((0,), (0,))
MIB = 1024 * 1024


def dot(a, b, dims=((1,), (0,))):
    return lax.dot_general(a, b, (dims, ((), ())), preferred_element_type=F32)


def fold_matrix(transposed=False):
    size = GROUP * PARTS
    row = lax.broadcasted_iota(jnp.int32, (size, size), 0)
    col = lax.broadcasted_iota(jnp.int32, (size, size), 1)
    if transposed:
        row, col = col, row
    return (col == (row % GROUP) * PARTS + row // GROUP).astype(F32).astype(BF)


def unfold(folded, rows_ref):
    order = fold_matrix()
    for first in range(0, EXPERTS, GROUP):
        flat = dot(order, folded[first * PARTS:(first + GROUP) * PARTS, :]).astype(BF)
        for i in range(PARTS):
            for f in range(RCAP):
                at = f * EXPERTS + first
                rows_ref[at:at + GROUP, i * PIECE:(i + 1) * PIECE] = flat[
                    i * GROUP:(i + 1) * GROUP, f * PIECE:(f + 1) * PIECE
                ]


def fold(rows, folded_ref):
    order = fold_matrix(transposed=True)
    for first in range(0, EXPERTS, GROUP):
        flat = jnp.concatenate(
            [
                jnp.concatenate(
                    [
                        rows[f * EXPERTS + first:f * EXPERTS + first + GROUP,
                             i * PIECE:(i + 1) * PIECE]
                        for f in range(RCAP)
                    ],
                    axis=1,
                )
                for i in range(PARTS)
            ],
            axis=0,
        )
        folded_ref[first * PARTS:(first + GROUP) * PARTS, :] = dot(order, flat).astype(BF)


def home_picks(slots, scale=None):
    s = lax.broadcasted_iota(jnp.int32, (EXPERTS, CAP, TOK), 1).astype(F32) + 1.0
    value = F32(1.0) if scale is None else scale[:EXPERTS][:, None, :]
    return jnp.where(slots[:EXPERTS][:, None, :] == s, value, 0.0).reshape(HOME, TOK)


def far_picks(slots, scale=None):
    value = F32(1.0) if scale is None else scale[EXPERTS:]
    return jnp.concatenate(
        [jnp.where(slots[EXPERTS:] == F32(f + 1), value, 0.0) for f in range(RCAP)], axis=0
    )


def split(values):
    high = values.astype(BF)
    return high, (values - high.astype(F32)).astype(BF)


def plan_kernel(me_ref, hot_hbm, holder_hbm, cap_hbm, routes_hbm, weight_hbm, pick_hbm, tokens_hbm,
                send_hbm, slots_ref, scale_ref, hot_ref, holder_ref, cap_ref, routes_ref,
                weight_ref, pick_ref, tokens_ref, send_ref, later_ref, sems, out_sems):
    copies = [
        pltpu.make_async_copy(src, dst, sems.at[i])
        for i, (src, dst) in enumerate(
            (
                (hot_hbm, hot_ref), (holder_hbm, holder_ref), (cap_hbm, cap_ref),
                (routes_hbm, routes_ref), (pick_hbm, pick_ref), (weight_hbm, weight_ref),
                (tokens_hbm, tokens_ref),
            )
        )
    ]
    for copy in copies:
        copy.start()
    later_ref[...] = jnp.ones(later_ref.shape, F32)

    def turn(step, carry):
        value = later_ref[...]
        for _ in range(8):
            value = value * 0.5 + 1.0
        later_ref[...] = value
        return carry

    lax.fori_loop(0, me_ref[0] * LATER, turn, 0)
    for copy in copies[:-1]:
        copy.wait()
    lane = lax.broadcasted_iota(jnp.int32, (1, TOK), 1)
    limit = jnp.zeros((1, TOK), jnp.int32)
    for e in range(EXPERTS):
        limit = jnp.where(lane == e, cap_ref[e], limit)
    hot = jnp.zeros((1, TOK), jnp.int32)
    for j in range(HOT):
        hot = jnp.where(lane % EXPERTS == hot_ref[j], 1, hot)
        limit = jnp.where(
            lane == EXPERTS + hot_ref[j], jnp.minimum(cap_ref[holder_ref[j]], RCAP), limit
        )
    row = lax.broadcasted_iota(jnp.int32, (TOK, TOK), 0)
    col = lax.broadcasted_iota(jnp.int32, (TOK, TOK), 1)
    limit = jnp.sum(jnp.where(row == col, limit, 0), axis=1, keepdims=True)
    hot = jnp.sum(jnp.where(row == col, hot, 0), axis=1, keepdims=True)
    expert = row % EXPERTS
    far_class = row // EXPERTS
    present = jnp.zeros((TOK, TOK), F32)
    scale = jnp.zeros((TOK, TOK), jnp.int32)
    for k in range(TOPK):
        replica = hot * pick_ref[k:k + 1, :]
        match = jnp.logical_and(routes_ref[k:k + 1, :] == expert, replica == far_class)
        present = jnp.where(match, 1.0, present)
        scale = jnp.where(match, weight_ref[k:k + 1, :], scale)
    rank = dot(present.astype(BF), (row < col).astype(F32).astype(BF))
    kept = jnp.logical_and(present > 0.0, rank < limit.astype(F32))
    slots = jnp.where(kept, rank + 1.0, 0.0)
    slots_ref[...] = slots
    scale_ref[...] = scale.astype(F32) * (1.0 / 4096.0)
    home = home_picks(slots).astype(BF)
    copies[-1].wait()
    sends = []
    for n in range(4):
        cols = slice(n * 2 * STEP, (n + 1) * 2 * STEP)
        send_ref[:, cols] = dot(home, tokens_ref[:, cols]).astype(BF)
        sends.append(
            pltpu.make_async_copy(send_ref.at[:, cols], send_hbm.at[:, cols], out_sems.at[n])
        )
        sends[-1].start()
    fold(dot(far_picks(slots).astype(BF), tokens_ref[...]).astype(BF), send_ref.at[:, D:])
    sends.append(
        pltpu.make_async_copy(send_ref.at[:, D:], send_hbm.at[:, D:], out_sems.at[len(sends)])
    )
    sends[-1].start()
    for copy in sends:
        copy.wait()


def grads_kernel(slots_ref, scale_ref, cot_ref, send_ref, both_ref):
    slots, scale = slots_ref[...], scale_ref[...]
    both_ref[:TOK, :] = cot_ref[...]
    both_ref[TOK:, :] = cot_ref[...]
    home = jnp.concatenate(split(home_picks(slots, scale)), axis=1)
    for c in range(0, D, 2 * STEP):
        cols = slice(c, c + 2 * STEP)
        send_ref[:, cols] = dot(home, both_ref[:, cols]).astype(BF)
    far = jnp.concatenate(split(far_picks(slots, scale)), axis=1)
    fold(dot(far, both_ref[...]).astype(BF), send_ref.at[:, D:])


ACROSS = ((1,), (1,))
BLOCKS = ((HOME, FAR), (0, HOME // 2), (HOME // 2, HOME // 2))


def forward_kernel(got_ref, gate_ref, up_ref, down_ref, send_ref, far_ref, hidden_ref,
                   gate_factor_ref, up_factor_ref):
    unfold(got_ref[:, D:], far_ref)
    for first, count in BLOCKS:
        here = slice(first, first + count)
        x = far_ref[...] if first == HOME else got_ref[here, :D]
        pre_gate = dot(x, gate_ref[...])
        pre_up = dot(x, up_ref[...])
        sigma = jax.nn.sigmoid(pre_gate)
        active = pre_gate * sigma
        gate_factor_ref[here, :] = pre_up * sigma * (1.0 + pre_gate * (1.0 - sigma))
        up_factor_ref[here, :] = active
        hidden = (active * pre_up).astype(BF)
        hidden_ref[here, :] = hidden
        out = dot(hidden, down_ref[...], ACROSS).astype(BF)
        if first == HOME:
            fold(out, send_ref.at[:, D:])
        else:
            send_ref[here, :D] = out


def backward_kernel(got_ref, gate_ref, up_ref, down_ref, gate_factor_ref, up_factor_ref, send_ref,
                    far_ref, back_gate_ref, back_up_ref):
    unfold(got_ref[:, D:], far_ref)
    for first, count in BLOCKS:
        here = slice(first, first + count)
        g = far_ref[...] if first == HOME else got_ref[here, :D]
        back_hidden = dot(g, down_ref[...])
        back_gate = (back_hidden * gate_factor_ref[here, :]).astype(BF)
        back_up = (back_hidden * up_factor_ref[here, :]).astype(BF)
        back_gate_ref[here, :] = back_gate
        back_up_ref[here, :] = back_up
        back = dot(back_gate, gate_ref[...], ACROSS) + dot(back_up, up_ref[...], ACROSS)
        if first == HOME:
            fold(back.astype(BF), send_ref.at[:, D:])
        else:
            send_ref[here, :D] = back.astype(BF)


def weight_kernel(me_ref, home_ref, far_ref, *refs):
    count = len(refs) // 3
    backs, sends, keeps = refs[:count], refs[count:2 * count], refs[2 * count:]
    for half, grads in ((1 - me_ref[0], sends), (me_ref[0], keeps)):

        def step(n, carry, half=half, grads=grads):
            rows = pl.ds(pl.multiple_of(n * STEP, STEP), STEP)
            cols = pl.ds(pl.multiple_of(half * HALF + n * STEP, STEP), STEP)
            home, far = home_ref[:, cols], far_ref[:, cols]
            for back, grad in zip(backs, grads):
                total = dot(home, back[:HOME, :], TURN) + dot(far, back[HOME:, :], TURN)
                grad[rows, :] = total.astype(BF)
            return carry

        lax.fori_loop(0, HALF // STEP, step, 0)


def ones_kernel(slots_ref, home_ones_ref, far_ones_ref):
    home_ones_ref[...] = home_picks(slots_ref[...]).T.astype(BF)
    far_ones_ref[...] = far_picks(slots_ref[...]).T.astype(BF)


def mixed_kernel(slots_ref, scale_ref, got_ref, mixed_ref, far_ref):
    unfold(got_ref[:, D:], far_ref)
    slots, scale = slots_ref[...], scale_ref[...]
    home = jnp.concatenate(split(home_picks(slots, scale)), axis=1)
    far = jnp.concatenate(split(far_picks(slots, scale)), axis=1)
    for c in range(0, D, STEP):
        cols = slice(c, c + STEP)
        both = dot(home, got_ref[:, cols], TURN) + dot(far, far_ref[:, cols], TURN)
        mixed_ref[:, cols] = (both[:TOK] + both[TOK:]).astype(BF)


def back_kernel(home_ref, far_ones_ref, got_ref, grad_ref, far_ref):
    unfold(got_ref[:, D:], far_ref)
    for c in range(0, D, 2 * STEP):
        cols = slice(c, c + 2 * STEP)
        grad_ref[:, cols] = (
            dot(home_ref[...], got_ref[:, cols]) + dot(far_ones_ref[...], far_ref[:, cols])
        ).astype(BF)


VMEM = pl.BlockSpec(memory_space=pltpu.VMEM)
SMEM = pl.BlockSpec(memory_space=pltpu.SMEM)
HBM = pl.BlockSpec(memory_space=pltpu.HBM)


def call(kernel, outs, args, flops, scratch=(), limit=32, in_specs=None, out_specs=None):
    size = sum(a.size * a.dtype.itemsize for a in args)
    size += sum(o.size * o.dtype.itemsize for o in outs)
    return pl.pallas_call(
        kernel,
        out_shape=outs,
        in_specs=in_specs or [VMEM] * len(args),
        out_specs=out_specs or [VMEM] * len(outs),
        scratch_shapes=list(scratch),
        compiler_params=pltpu.CompilerParams(vmem_limit_bytes=limit * MIB),
        cost_estimate=pl.CostEstimate(flops=flops, bytes_accessed=size, transcendentals=0),
    )(*args)


def shape(rows, cols, dtype=BF):
    return jax.ShapeDtypeStruct((rows, cols), dtype)


def exchange(values):
    return lax.all_to_all(values, "expert", split_axis=0, concat_axis=0, tiled=True)


def shards(tokens, cotangent, routes, route_weight, replica_pick, hot_experts, hot_holders,
           capacity, gate_weight, up_weight, down_weight):
    gate, up, down = gate_weight[0], up_weight[0], down_weight[0]
    product = 2 * ROWS * D * FF
    move = 2 * ROWS * TOK * D
    square = shape(TOK, TOK, F32)
    packed, far = shape(HOME, WIDE), shape(FAR, D)
    act, act32 = shape(ROWS, FF), shape(ROWS, FF, F32)
    far_scratch = pltpu.VMEM((FAR, D), BF)
    dma = pltpu.SemaphoreType.DMA

    me = lax.axis_index("dp").reshape(1)
    send_x, slots, scale = call(
        plan_kernel,
        [packed, square, square],
        (me, hot_experts, hot_holders, capacity, routes.T, route_weight.T, replica_pick.T, tokens),
        move,
        [pltpu.SMEM((HOT,), jnp.int32), pltpu.SMEM((HOT,), jnp.int32),
         pltpu.SMEM((EXPERTS,), jnp.int32)]
        + [pltpu.VMEM((TOPK, TOK), jnp.int32)] * 3
        + [pltpu.VMEM((TOK, D), BF), pltpu.VMEM((HOME, WIDE), BF), pltpu.VMEM((8, TOK), F32), dma((7,)), dma((5,))],
        60,
        [SMEM] + [HBM] * 7,
        [HBM, VMEM, VMEM],
    )
    got_x = exchange(send_x)
    cotangent, got_x = lax.optimization_barrier((cotangent, got_x))
    (send_g,) = call(
        grads_kernel, [packed], (slots, scale, cotangent), 2 * move,
        [pltpu.VMEM((2 * TOK, D), BF)],
    )
    got_g = exchange(send_g)
    send_out, far_x, hidden, gate_factor, up_factor = call(
        forward_kernel, [packed, far, act, act32, act32], (got_x, gate, up, down), 3 * product
    )
    slots_later, got_g = lax.optimization_barrier((slots, got_g))
    home_ones, far_ones = call(
        ones_kernel, [shape(TOK, HOME), shape(TOK, FAR)], (slots_later,), move // 16, limit=16
    )
    send_out, home_ones = lax.optimization_barrier((send_out, home_ones))
    got_out = exchange(send_out)
    send_back, far_g, back_gate, back_up = call(
        backward_kernel, [packed, far, act, act],
        (got_g, gate, up, down, gate_factor, up_factor), 3 * product, limit=60,
    )
    send_back, got_out = lax.optimization_barrier((send_back, got_out))
    got_back = exchange(send_back)
    half = shape(HALF, FF)
    send_down, keep_down = call(
        weight_kernel, [half] * 2, (me, got_g, far_g, hidden), product, limit=20,
        in_specs=[SMEM] + [VMEM] * 3,
    )
    send_gate, send_up, keep_gate, keep_up = call(
        weight_kernel, [half] * 4, (me, got_x, far_x, back_gate, back_up), 2 * product,
        limit=20,
        in_specs=[SMEM] + [VMEM] * 4,
    )
    grads = [
        (keep.astype(F32) + lax.ppermute(sent, "dp", ((0, 1), (1, 0))).astype(F32)).astype(BF)[None]
        for sent, keep in ((send_gate, keep_gate), (send_up, keep_up), (send_down, keep_down))
    ]
    (mixed,) = call(
        mixed_kernel, [shape(TOK, D)], (slots, scale, got_out),
        2 * move, [far_scratch], 16,
    )
    (grad_tokens,) = call(
        back_kernel, [shape(TOK, D)], (home_ones, far_ones, got_back), move, [far_scratch], 16
    )
    return (mixed, grad_tokens, *grads)


def solution(mesh):
    tokens = P(("dp", "expert"), None)
    weights = P("expert", None, None)
    grads = P("expert", "dp", None)
    return jax.shard_map(
        shards,
        mesh=mesh,
        in_specs=(tokens,) * 5 + (P(),) * 3 + (weights,) * 3,
        out_specs=(tokens, tokens, grads, grads, grads),
        check_vma=False,
    )
```
